32 devices in a mesh: grp: 2 (over y), row: 4 (over z), col: 4 (over x, core).
Axes of the slice: x: 2, y: 2, z: 4, core: 2. Of those that a mesh axis runs over, the one named last changes fastest.
Arguments:
- pair_track: bfloat16 [64, 32, 128], P(('grp', 'row'), 'col'), parts along dimension 0, may hold values from -6 to 6
- pair_mask: int32 [64, 32], P(('grp', 'row'), 'col'), parts along dimension 0, may hold values from 0 to 1, as said below
- token_mask: int32 [64], P('grp'), parts along dimension 0, may hold values from 0 to 1, as said below
- mult_gate: bfloat16 [128, 256], replicated, may hold values from -0.5 to 0.5
- mult_value: bfloat16 [128, 256], replicated, may hold values from -0.5 to 0.5
- mult_outgate: bfloat16 [128, 128], replicated, may hold values from -0.5 to 0.5
- mult_outproj: bfloat16 [128, 128], replicated, may hold values from -0.5 to 0.5
- attn_proj: bfloat16 [128, 512], replicated, may hold values from -0.5 to 0.5
- attn_bias: bfloat16 [128, 4], replicated, may hold values from -44 to 44
- attn_outproj: bfloat16 [128, 128], replicated, may hold values from -0.5 to 0.5
- trans_gate: bfloat16 [128, 512], replicated, may hold values from -0.5 to 0.5
- trans_value: bfloat16 [128, 512], replicated, may hold values from -0.5 to 0.5
- trans_outproj: bfloat16 [512, 128], replicated, may hold values from -0.25 to 0.25
Outputs:
- pair_out: bfloat16 [64, 32, 128], P(('grp', 'row', 'col')), parts along dimension 0
The draws below stay inside these ranges and needn't reach their ends.
There are 2 independent parts, one for each index of `grp`. The reference program is written for one: setup_inputs(seed, part) draws one part's arguments, and reference() takes and returns one part's arrays. A program takes and returns all parts, laid end to end along the dimension named above; an argument that names none is the same for every part. Nothing has to cross between parts.
Inputs may be any that keep to these rules, and one draw needn't show every extreme that they name: pair_mask[i, 0] and pair_mask[i, i] are 1 for every i. token_mask is 1 on a leading run of at least 24 tokens and 0 after it; at least the last token is 0.
All inputs are finite; a program needn't handle non-finite values.
Results may differ from the reference program's by a relative error of at most 0.015.
The reference program's roundings to bfloat16 on the way count: a program that leaves them out, or rounds other values in their place, can miss the bound.
Values may be sent and summed in bfloat16 or wider, within the bound.
No kernel may reach another device: no remote copies, remote signals or barrier semaphores. Data moves between devices by JAX's collectives and lax.ppermute only.
A program may use at most 64 MiB of HBM per device.

```python
import math
import jax
import jax.numpy as jnp
from jax import lax

C = 128
CMUL = 128
HEADS = 4
HDIM = 32
FF = 512
N = 32


def draw_pair_mask(key, part):
    key = jax.random.fold_in(key, 11)
    random_bits = jax.random.randint(key, (N, N), 0, 8)
    keep_mask = (random_bits > 0).astype(jnp.int32)
    row_index = lax.broadcasted_iota(jnp.int32, (N, N), 0)
    col_index = lax.broadcasted_iota(jnp.int32, (N, N), 1)
    forced = (col_index == 0) | (col_index == row_index)
    return jnp.where(forced, 1, keep_mask).astype(jnp.int32)


def draw_token_mask(key, part):
    key = jax.random.fold_in(key, 23)
    quarter = N // 4
    offset = jax.random.randint(key, (), 0, quarter)
    live_count = N - quarter + (offset + part) % quarter
    return (jnp.arange(N, dtype=jnp.int32) < live_count).astype(jnp.int32)


def draw_attn_bias(key, part):
    key = jax.random.fold_in(key, 37)
    uniform_part = jax.random.uniform(key, (C, HEADS), jnp.float32, -1.0, 1.0) * math.sqrt(3.0)
    return (uniform_part * 1.5 / math.sqrt(C)).astype(jnp.bfloat16)


def block_scale(rng, dims, shards, low, top_value):
    loudness = 1.0
    for dim, parts in shards:
        draws = jax.random.uniform(jax.random.fold_in(jax.random.fold_in(rng, 6), dim), (parts,), jnp.float32, low / len(shards), top_value / len(shards))
        loudness = loudness * jnp.repeat(jnp.exp(draws), dims[dim] // parts).reshape((-1,) + (1,) * (len(dims) - 1 - dim))
    return loudness


def gaussian(key, dims, deviation, limit, split=(), kind=jnp.bfloat16):
    drawn = deviation * jax.random.normal(key, dims, jnp.float32)
    if split:
        drawn = drawn * block_scale(key, dims, split, -0.22, 0.18)
    return jnp.clip(drawn, -limit, limit).astype(kind)


def setup_inputs(seed: int = 0, part: int = 0) -> dict:
    key_list = jax.random.split(jax.random.key(seed), 14)
    part_keys = jax.random.split(jax.random.fold_in(key_list[13], part), 14)
    pair_track = gaussian(part_keys[0], (N, N, C), 1.0, 6.0, ((0, 4), (1, 4)))
    pair_mask = draw_pair_mask(jax.random.fold_in(jax.random.fold_in(key_list[13], part), 71), part)
    token_mask = draw_token_mask(jax.random.fold_in(jax.random.fold_in(key_list[13], part), 71), part)
    mult_gate = gaussian(key_list[3], (C, 2 * CMUL), C ** -0.5, 0.5)
    mult_value = gaussian(key_list[4], (C, 2 * CMUL), C ** -0.5, 0.5)
    mult_outgate = gaussian(key_list[5], (C, C), C ** -0.5, 0.5)
    mult_outproj = gaussian(key_list[6], (CMUL, C), CMUL ** -0.5, 0.5)
    attn_proj = gaussian(key_list[7], (C, 4 * HEADS * HDIM), C ** -0.5, 0.5)
    attn_bias = draw_attn_bias(jax.random.fold_in(key_list[13], 71), part)
    attn_outproj = gaussian(key_list[9], (HEADS * HDIM, C), (HEADS * HDIM) ** -0.5, 0.5)
    trans_gate = gaussian(key_list[10], (C, FF), C ** -0.5, 0.5)
    trans_value = gaussian(key_list[11], (C, FF), C ** -0.5, 0.5)
    trans_outproj = gaussian(key_list[12], (FF, C), FF ** -0.5, 0.25)
    return {"pair_track": pair_track, "pair_mask": pair_mask, "token_mask": token_mask, "mult_gate": mult_gate, "mult_value": mult_value, "mult_outgate": mult_outgate, "mult_outproj": mult_outproj, "attn_proj": attn_proj, "attn_bias": attn_bias, "attn_outproj": attn_outproj, "trans_gate": trans_gate, "trans_value": trans_value, "trans_outproj": trans_outproj}


epsilon = 1e-05
masked_score = -1000000000.0

def normalize(values, axis):
    widened = values.astype(jnp.float32)
    center = widened - lax.optimization_barrier(jnp.mean(widened, axis=axis, keepdims=True))
    spread = lax.optimization_barrier(jnp.mean(center * center, axis=axis, keepdims=True))
    return center * lax.rsqrt(spread + epsilon)

def project(normed, weight):
    return jnp.einsum('ijc,cd->ijd', normed.astype(jnp.float32), weight.astype(jnp.float32))

def reference(pair_track, pair_mask, token_mask, mult_gate, mult_value, mult_outgate, mult_outproj, attn_proj, attn_bias, attn_outproj, trans_gate, trans_value, trans_outproj):
    token_rows = token_mask.astype(jnp.float32)
    key_mask = pair_mask.astype(jnp.float32) * token_rows[None, :]
    mult_mask = key_mask * token_rows[:, None]
    residual = pair_track.astype(jnp.float32)
    normed = normalize(pair_track, 2).astype(jnp.bfloat16)
    paired = jax.nn.sigmoid(project(normed, mult_gate)) * project(normed, mult_value) * mult_mask[:, :, None]
    paired = paired.astype(jnp.bfloat16)
    left_side = paired[:, :, :CMUL].astype(jnp.float32)
    right_side = paired[:, :, CMUL:].astype(jnp.float32)
    crossed = jnp.einsum('ikc,jkc->ijc', left_side, right_side).astype(jnp.bfloat16)
    mixed_norm = normalize(crossed, 2).astype(jnp.bfloat16)
    outgate = jax.nn.sigmoid(project(normed, mult_outgate))
    residual = residual + outgate * project(mixed_norm, mult_outproj)
    normed = normalize(residual, 2).astype(jnp.bfloat16)
    inner_width = HEADS * HDIM
    projected = project(normed, attn_proj)
    queries = (projected[:, :, :inner_width] * HDIM ** (-0.5)).astype(jnp.bfloat16).reshape(N, N, HEADS, HDIM)
    key_rows = projected[:, :, inner_width:2 * inner_width].astype(jnp.bfloat16).reshape(N, N, HEADS, HDIM)
    value_rows = projected[:, :, 2 * inner_width:3 * inner_width].astype(jnp.bfloat16).reshape(N, N, HEADS, HDIM)
    gating = jax.nn.sigmoid(projected[:, :, 3 * inner_width:])
    bias = jnp.einsum('jkc,ch->hjk', normed.astype(jnp.float32), attn_bias.astype(jnp.float32)).astype(jnp.bfloat16)

    def one_row(row_args):
        query_row, key_row, value_row, gate_row, allowed = row_args
        scores = jnp.einsum('jhd,khd->hjk', query_row.astype(jnp.float32), key_row.astype(jnp.float32))
        scores = scores + bias.astype(jnp.float32)
        scores = jnp.where(allowed[None, None, :], scores, masked_score)
        row_max = lax.optimization_barrier(jnp.max(scores, axis=2, keepdims=True))
        expo = jnp.exp(scores - row_max)
        attn_weights = (expo / lax.optimization_barrier(jnp.sum(expo, axis=2, keepdims=True))).astype(jnp.bfloat16)
        summed = jnp.einsum('hjk,khd->jhd', attn_weights.astype(jnp.float32), value_row.astype(jnp.float32))
        gated_out = (gate_row * summed.reshape(N, inner_width)).astype(jnp.bfloat16)
        return jnp.dot(gated_out, attn_outproj, preferred_element_type=jnp.float32)
    attended = lax.map(one_row, (queries, key_rows, value_rows, gating, key_mask > 0.5))
    residual = residual + attended
    normed = normalize(residual, 2).astype(jnp.bfloat16)
    transit = (jax.nn.silu(project(normed, trans_gate)) * project(normed, trans_value)).astype(jnp.bfloat16)
    residual = residual + project(transit, trans_outproj)
    return residual.astype(jnp.bfloat16)
```

```python
import functools

import jax
import jax.numpy as jnp
from jax import lax
from jax.experimental import pallas as pl
from jax.experimental.pallas import tpu as pltpu
from jax.sharding import PartitionSpec as P

epsilon = 1e-05
masked_score = -1000000000.0
crop_axes = ("row", "col")
lanes = 128
crop_bytes_max = 1 << 20


def layer_norm(values):
    center = values - jnp.mean(values, axis=-1, keepdims=True)
    spread = jnp.mean(center * center, axis=-1, keepdims=True)
    return center * lax.rsqrt(spread + epsilon)


def sigmoid(values):
    return 1.0 / (1.0 + jnp.exp(-values))


def dot(left, right):
    return jnp.dot(left, right, preferred_element_type=jnp.float32)


def pack_kernel(track_ref, mask_ref, out_ref):
    block_rows, block_cols = mask_ref.shape
    pairs = block_rows * block_cols
    width = out_ref.shape[1]
    out_ref[:pairs, :] = track_ref[...]
    below = out_ref.shape[0] - pairs
    mask = mask_ref[...].astype(jnp.float32)
    pick = (
        lax.broadcasted_iota(jnp.int32, (below, block_cols), 0)
        == lax.broadcasted_iota(jnp.int32, (below, block_cols), 1)
    ).astype(jnp.float32)
    place = (
        lax.broadcasted_iota(jnp.int32, (block_rows, width), 0)
        == lax.broadcasted_iota(jnp.int32, (block_rows, width), 1)
    ).astype(jnp.float32)
    turned = lax.dot_general(mask, place, (((0,), (0,)), ((), ())), preferred_element_type=jnp.float32)
    out_ref[pairs:, :] = dot(pick, turned).astype(out_ref.dtype)


def crop_kernel(
    offsets,
    col_count,
    me_ref,
    tokens_ref,
    crop_ref,
    token_col_ref,
    mult_gate_ref,
    mult_value_ref,
    mult_outgate_ref,
    mult_outproj_ref,
    attn_proj_ref,
    bias_wide_ref,
    attn_outproj_ref,
    trans_gate_ref,
    trans_value_ref,
    trans_outproj_ref,
    out_ref,
    track,
    normed,
    key_wide,
    mult_wide,
    left,
    right,
    outgate,
    bias,
):
    length = tokens_ref.shape[0]
    channels = track.shape[2]
    hidden = mult_outproj_ref.shape[0]
    own_rows = out_ref.shape[0] // length
    inner = attn_outproj_ref.shape[0]
    spans = bias_wide_ref.shape[1]
    heads = spans // length
    head_width = inner // heads
    block_rows = length // (len(offsets) // col_count)
    block_cols = length // col_count
    pairs = block_rows * block_cols
    me = me_ref[0]

    token_col = token_col_ref[...]
    for slot, offset in enumerate(offsets):
        block = me ^ offset
        first_row = (block // col_count) * block_rows
        cols = pl.ds(pl.multiple_of((block % col_count) * block_cols, block_cols), block_cols)
        values = crop_ref[slot, :pairs, :].astype(jnp.float32)
        turned = crop_ref[slot, pairs:, :].astype(jnp.float32)[:block_cols]
        rounded = layer_norm(values)
        values = values.reshape(block_rows, block_cols, channels)
        rounded = rounded.reshape(block_rows, block_cols, channels)
        tokens = token_col_ref[cols, :]
        for row in range(block_rows):
            key = turned[:, row : row + 1] * tokens
            track[first_row + row, cols, :] = values[row]
            normed[first_row + row, cols, :] = rounded[row]
            key_wide[first_row + row, cols, :] = key
            mult_wide[first_row + row, cols, :] = key * tokens_ref[first_row + row].astype(jnp.float32)

    step = block_rows
    steps = length // step

    @pl.loop(0, steps)
    def _(index):
        rows = pl.ds(index * step, step)
        flat = pl.ds(pl.multiple_of(index * step * length, step * length), step * length)
        source = normed[rows].reshape(step * length, channels).astype(jnp.bfloat16)
        mask = mult_wide[rows].reshape(step * length, lanes)
        paired = sigmoid(dot(source, mult_gate_ref[...])) * dot(source, mult_value_ref[...])
        left[flat, :] = (paired[:, :hidden] * mask).astype(jnp.bfloat16).astype(jnp.float32)
        right[flat, :] = (paired[:, hidden:] * mask).astype(jnp.bfloat16).astype(jnp.float32)
        outgate[flat, :] = sigmoid(dot(source, mult_outgate_ref[...]))

    head_of_lane = lax.broadcasted_iota(jnp.int32, (1, spans), 1) // length
    key_of_lane = lax.broadcasted_iota(jnp.int32, (length, spans), 1) % length
    on_key = (lax.broadcasted_iota(jnp.int32, (length, spans), 0) == key_of_lane).astype(jnp.float32)

    def spread_keys(values):
        values = values.reshape(values.shape[0] // length, length, spans)
        return jnp.sum(values * on_key[None], axis=1)

    @pl.loop(0, steps)
    def _(index):
        flat = pl.ds(pl.multiple_of(index * step * length, step * length), step * length)
        total = [jnp.zeros((length, hidden), jnp.float32) for _ in range(step)]
        for k in range(length):
            column = right[pl.ds(k, length, stride=length), :]
            for i in range(step):
                total[i] = total[i] + left[pl.ds((index * step + i) * length + k, 1), :] * column
        crossed = jnp.concatenate(total, axis=0).astype(jnp.bfloat16).astype(jnp.float32)
        mixed = layer_norm(crossed).astype(jnp.bfloat16)
        update = outgate[flat, :] * dot(mixed, mult_outproj_ref[...])
        rows = pl.ds(index * step, step)
        after = track[rows].reshape(step * length, channels) + update
        again = layer_norm(after)
        track[rows] = after.reshape(step, length, channels)
        normed[rows] = again.reshape(step, length, channels)
        wide = dot(again.astype(jnp.bfloat16), bias_wide_ref[...])
        wide = wide.astype(jnp.bfloat16).astype(jnp.float32)
        bias[rows, :] = spread_keys(wide)

    own = pl.ds(me * own_rows, own_rows)
    residual = track[own].reshape(own_rows * length, channels)
    source = normed[own].reshape(own_rows * length, channels).astype(jnp.bfloat16)
    projected = dot(source, attn_proj_ref[...])
    queries = (projected[:, :inner] * head_width ** (-0.5)).astype(jnp.bfloat16)
    keys = projected[:, inner : 2 * inner]
    values = projected[:, 2 * inner : 3 * inner]
    gating = sigmoid(projected[:, 3 * inner :])
    allowed = spread_keys(key_wide[own].reshape(own_rows * length, spans)) > 0.5
    head_of_row = lax.broadcasted_iota(jnp.int32, (spans, inner), 0) // length
    head_of_channel = lax.broadcasted_iota(jnp.int32, (spans, inner), 1) // head_width
    same_head = (head_of_row == head_of_channel).astype(jnp.float32)
    gathered = []
    for row in range(own_rows):
        here = slice(row * length, (row + 1) * length)
        tall_keys = (jnp.concatenate([keys[here]] * heads, axis=0) * same_head).astype(jnp.bfloat16)
        tall_values = (jnp.concatenate([values[here]] * heads, axis=0) * same_head).astype(jnp.bfloat16)
        scores = lax.dot_general(
            queries[here], tall_keys, (((1,), (1,)), ((), ())), preferred_element_type=jnp.float32
        )
        scores = jnp.where(allowed[row : row + 1], scores + bias[...], masked_score)
        top = jnp.zeros_like(scores)
        for head in range(heads):
            here_lanes = head_of_lane == head
            most = jnp.max(jnp.where(here_lanes, scores, -jnp.inf), axis=1, keepdims=True)
            top = jnp.where(here_lanes, most, top)
        expo = jnp.exp(scores - top)
        whole = jnp.zeros_like(scores)
        for head in range(heads):
            here_lanes = head_of_lane == head
            part = jnp.sum(jnp.where(here_lanes, expo, 0.0), axis=1, keepdims=True)
            whole = jnp.where(here_lanes, part, whole)
        gathered.append(dot((expo / whole).astype(jnp.bfloat16), tall_values))
    gated = (gating * jnp.concatenate(gathered, axis=0)).astype(jnp.bfloat16)
    residual = residual + dot(gated, attn_outproj_ref[...])
    source = layer_norm(residual).astype(jnp.bfloat16)
    gate = dot(source, trans_gate_ref[...])
    transit = (gate * sigmoid(gate) * dot(source, trans_value_ref[...])).astype(jnp.bfloat16)
    out_ref[...] = (residual + dot(transit, trans_outproj_ref[...])).astype(out_ref.dtype)


def gathered_crop(
    pair_track,
    pair_mask,
    token_mask,
    mult_gate,
    mult_value,
    mult_outgate,
    mult_outproj,
    attn_proj,
    attn_bias,
    attn_outproj,
    trans_gate,
    trans_value,
    trans_outproj,
):
    row_count, col_count = lax.axis_size("row"), lax.axis_size("col")
    devices = row_count * col_count
    block_rows, block_cols, channels = pair_track.shape
    length = block_cols * col_count
    pairs = block_rows * block_cols
    own_rows = length // devices
    me = lax.axis_index(crop_axes)
    in_vmem = pl.BlockSpec(memory_space=pltpu.VMEM)
    in_smem = pl.BlockSpec(memory_space=pltpu.SMEM)
    block = pl.pallas_call(
        pack_kernel,
        out_shape=jax.ShapeDtypeStruct((pairs + 16, channels), pair_track.dtype),
        in_specs=[in_vmem, in_vmem],
        out_specs=in_vmem,
        name="pack",
    )(pair_track.reshape(pairs, channels), pair_mask)
    crop = block[None]
    offsets = [0]
    mask = devices // 2
    while mask:
        turn = mask | 1
        crop = jnp.concatenate(
            [crop, lax.ppermute(crop, crop_axes, [(i, i ^ turn) for i in range(devices)])]
        )
        offsets = offsets + [offset ^ turn for offset in offsets]
        mask //= 2
    heads = attn_bias.shape[1]
    token_col = jnp.broadcast_to(token_mask.astype(jnp.float32)[:, None], (length, lanes))
    bias_wide = jnp.repeat(attn_bias, length, axis=1)
    whole = pltpu.VMEM((length, length, channels), jnp.float32)
    flat = pltpu.VMEM((length * length, channels), jnp.float32)
    out = pl.pallas_call(
        functools.partial(crop_kernel, tuple(offsets), col_count),
        out_shape=jax.ShapeDtypeStruct((own_rows * length, channels), jnp.bfloat16),
        in_specs=[in_smem, in_smem] + [in_vmem] * 12,
        out_specs=in_vmem,
        scratch_shapes=[whole, whole, whole, whole, flat, flat, flat, pltpu.VMEM((length, heads * length), jnp.float32)],
        compiler_params=pltpu.CompilerParams(vmem_limit_bytes=48 << 20),
        name="crop",
    )(
        me.astype(jnp.int32)[None],
        token_mask,
        crop,
        token_col,
        mult_gate,
        mult_value,
        mult_outgate,
        mult_outproj,
        attn_proj,
        bias_wide,
        attn_outproj,
        trans_gate,
        trans_value,
        trans_outproj,
    )
    return out.reshape(own_rows, length, channels)


def normalize(values, axis):
    widened = values.astype(jnp.float32)
    center = widened - jnp.mean(widened, axis=axis, keepdims=True)
    spread = jnp.mean(center * center, axis=axis, keepdims=True)
    return center * lax.rsqrt(spread + epsilon)


def project(normed, weight):
    return jnp.einsum("rkc,cd->rkd", normed, weight, preferred_element_type=jnp.float32)


def split_crop(
    pair_track,
    pair_mask,
    token_mask,
    mult_gate,
    mult_value,
    mult_outgate,
    mult_outproj,
    attn_proj,
    attn_bias,
    attn_outproj,
    trans_gate,
    trans_value,
    trans_outproj,
):
    col_count = lax.axis_size("col")
    rows_here = pair_track.shape[0] // col_count
    full_rows, full_mask = (
        lax.all_to_all(pair_track, "col", split_axis=0, concat_axis=1, tiled=True),
        lax.all_to_all(
            pair_mask.astype(jnp.bfloat16), "col", split_axis=0, concat_axis=1, tiled=True
        ),
    )
    length = full_rows.shape[1]
    row_start = (lax.axis_index("row") * col_count + lax.axis_index("col")) * rows_here
    token_rows = token_mask.astype(jnp.float32)
    own_tokens = lax.dynamic_slice_in_dim(token_rows, row_start, rows_here, 0)
    key_mask = full_mask.astype(jnp.float32) * token_rows[None, :]
    mult_mask = key_mask * own_tokens[:, None]
    residual = full_rows.astype(jnp.float32)
    normed = normalize(full_rows, 2).astype(jnp.bfloat16)
    gate_logit = jnp.einsum("rkc,cd->drk", normed, mult_gate, preferred_element_type=jnp.float32)
    value_part = jnp.einsum("rkc,cd->drk", normed, mult_value, preferred_element_type=jnp.float32)
    hidden = mult_gate.shape[1] // 2
    paired = (jax.nn.sigmoid(gate_logit) * value_part * mult_mask[None]).astype(jnp.bfloat16)
    paired = paired.reshape(2, hidden, rows_here, length)
    spread_pair = lax.all_to_all(paired, "col", split_axis=1, concat_axis=2, tiled=True)
    left_side = spread_pair[0]
    crossed = jnp.einsum(
        "cik,cjk->cij",
        left_side,
        lax.all_gather(spread_pair[1], "row", axis=1, tiled=True),
        preferred_element_type=jnp.float32,
    )
    crossed = crossed.astype(jnp.bfloat16)
    merged = lax.all_to_all(crossed, "col", split_axis=1, concat_axis=0, tiled=True)
    mixed_norm = normalize(merged, 0).astype(jnp.bfloat16)
    update = jnp.einsum("crk,cd->rkd", mixed_norm, mult_outproj, preferred_element_type=jnp.float32)
    outgate = jax.nn.sigmoid(project(normed, mult_outgate))
    residual = residual + outgate * update
    normed = normalize(residual, 2).astype(jnp.bfloat16)
    head_count = attn_bias.shape[1]
    inner_width = attn_outproj.shape[0]
    head_width = inner_width // head_count
    projected = project(normed, attn_proj)
    queries = (projected[:, :, :inner_width] * head_width ** (-0.5)).astype(jnp.bfloat16)
    queries = queries.reshape(rows_here, length, head_count, head_width)
    key_rows = (
        projected[:, :, inner_width : 2 * inner_width]
        .astype(jnp.bfloat16)
        .reshape(rows_here, length, head_count, head_width)
    )
    value_rows = (
        projected[:, :, 2 * inner_width : 3 * inner_width]
        .astype(jnp.bfloat16)
        .reshape(rows_here, length, head_count, head_width)
    )
    gating = jax.nn.sigmoid(projected[:, :, 3 * inner_width :])
    bias_local = jnp.einsum(
        "rkc,ch->hrk", normed, attn_bias, preferred_element_type=jnp.float32
    ).astype(jnp.bfloat16)
    allowed = key_mask > 0.5
    segment = lax.all_gather(bias_local, ("row", "col"), axis=1, tiled=True)
    amount = segment.shape[1]
    scores = jnp.einsum("rjhd,rkhd->hrjk", queries, key_rows, preferred_element_type=jnp.float32)
    scores = scores + segment.astype(jnp.float32)[:, None]
    scores = jnp.where(allowed[None, :, None, :], scores, masked_score)
    row_max = jnp.max(scores, axis=3, keepdims=True)
    expo = jnp.exp(scores - row_max)
    attn_weights = (expo / jnp.sum(expo, axis=3, keepdims=True)).astype(jnp.bfloat16)
    mixed_heads = jnp.einsum(
        "hrjk,rkhd->rjhd", attn_weights, value_rows, preferred_element_type=jnp.float32
    )
    gated_out = (gating * mixed_heads.reshape(rows_here, amount, inner_width)).astype(jnp.bfloat16)
    attended = jnp.einsum(
        "rjd,dc->rjc", gated_out, attn_outproj, preferred_element_type=jnp.float32
    )
    residual = residual + attended
    normed = normalize(residual, 2).astype(jnp.bfloat16)
    transit = (jax.nn.silu(project(normed, trans_gate)) * project(normed, trans_value)).astype(
        jnp.bfloat16
    )
    residual = residual + project(transit, trans_outproj)
    return residual.astype(jnp.bfloat16)


def on_device(pair_track, *others):
    devices = lax.axis_size("row") * lax.axis_size("col")
    pairs = pair_track.shape[0] * pair_track.shape[1] * devices
    heads = others[7].shape[1]
    length = pair_track.shape[1] * lax.axis_size("col")
    fits = pairs * pair_track.shape[2] * 4 <= crop_bytes_max
    if fits and heads * length == lanes and pair_track.shape[2] == lanes and devices & (devices - 1) == 0:
        return gathered_crop(pair_track, *others)
    return split_crop(pair_track, *others)


def solution(mesh):
    return jax.shard_map(
        on_device,
        mesh=mesh,
        in_specs=(
            P(("grp", "row"), "col", None),
            P(("grp", "row"), "col"),
            P("grp"),
            P(),
            P(),
            P(),
            P(),
            P(),
            P(),
            P(),
            P(),
            P(),
            P(),
        ),
        out_specs=P(("grp", "row", "col"), None, None),
        check_vma=False,
    )
```

```python
import functools

import jax
import jax.numpy as jnp
from jax import lax
from jax.experimental import pallas as pl
from jax.experimental.pallas import tpu as pltpu
from jax.sharding import PartitionSpec as P

epsilon = 1e-05
masked_score = -1000000000.0
crop_axes = ("row", "col")
lanes = 128
crop_bytes_max = 1 << 20


def dot(left, right):
    return jnp.dot(left, right, preferred_element_type=jnp.float32)


def sigmoid(values):
    return 1.0 / (1.0 + jnp.exp(-values))


def layer_norm(values):
    center = values - jnp.mean(values, axis=-1, keepdims=True)
    spread = jnp.mean(center * center, axis=-1, keepdims=True)
    return center * lax.rsqrt(spread + epsilon)


def slot_index(offset, devices):
    top = devices.bit_length() - 2
    slot = offset & 1
    for bit in range(1, top + 1):
        slot = slot ^ ((offset >> bit) & 1)
    slot = slot << top
    for bit in range(1, top + 1):
        slot = slot | (((offset >> bit) & 1) << (top - bit))
    return slot


def crop_kernel(
    slots,
    col_count,
    crop_ref,
    token_pair_ref,
    key_place_ref,
    mult_gate_ref,
    mult_value_ref,
    mult_outgate_ref,
    mult_outproj_ref,
    attn_proj_ref,
    bias_wide_ref,
    attn_outproj_ref,
    trans_gate_ref,
    trans_value_ref,
    trans_outproj_ref,
    out_ref,
    left,
    right,
    outgate,
    product,
    after,
    bias,
    key_lane,
):
    channels = after.shape[1]
    hidden = mult_outproj_ref.shape[0]
    inner = attn_outproj_ref.shape[0]
    length, spans = bias.shape
    heads = spans // length
    head_width = inner // heads
    own_rows = out_ref.shape[0] // length
    devices = len(slots)
    row_count = devices // col_count
    block_rows, block_cols = length // row_count, length // col_count
    pairs = block_rows * block_cols
    whole = length * length
    me = lax.axis_index(crop_axes)

    def slot_at(row, col):
        return slot_index((row * col_count + col) ^ me, devices)

    packed = crop_ref[:, :pairs, :].reshape(whole, channels)
    source = layer_norm(packed.astype(jnp.float32)).astype(jnp.bfloat16)
    diagonal = (
        lax.broadcasted_iota(jnp.int32, (block_cols, lanes), 0)
        == lax.broadcasted_iota(jnp.int32, (block_cols, lanes), 1)
    ).astype(jnp.float32)
    masks = []
    for slot, offset in enumerate(slots):
        mask = crop_ref[slot, pairs:, :].astype(jnp.float32)[:block_rows] * token_pair_ref[me ^ offset]
        masks.append((mask[:, None, :] * diagonal[None]).reshape(pairs, lanes))
    mask = dot(jnp.concatenate(masks, axis=0).astype(jnp.bfloat16), jnp.ones((lanes, channels), jnp.bfloat16))
    outgate[...] = sigmoid(dot(source, mult_outgate_ref[...]))
    paired = sigmoid(dot(source, mult_gate_ref[...])) * dot(source, mult_value_ref[...])
    left[...] = (paired[:, :hidden] * mask).astype(jnp.bfloat16).astype(jnp.float32)
    turned = (paired[:, hidden:] * mask).astype(jnp.bfloat16).astype(jnp.float32)
    for slot in range(devices):
        for row in range(block_rows):
            start = slot * pairs + row * block_cols
            right[pl.ds(slot * pairs + row, block_cols, stride=block_rows), :] = turned[start : start + block_cols]

    starts = [[slot_at(row, col) * pairs for col in range(col_count)] for row in range(row_count)]

    @pl.loop(0, row_count)
    def _(part):
        total = [jnp.zeros((length, hidden), jnp.float32) for _ in range(block_rows)]
        for col in range(col_count):
            start = slot_at(part, col) * pairs
            for k in range(block_cols):
                column = jnp.concatenate(
                    [
                        right[pl.ds(pl.multiple_of(starts[row][col] + k * block_rows, block_rows), block_rows), :]
                        for row in range(row_count)
                    ],
                    axis=0,
                )
                for row in range(block_rows):
                    total[row] = total[row] + left[pl.ds(start + row * block_cols + k, 1), :] * column
        step = block_rows * length
        product[pl.ds(pl.multiple_of(part * step, step), step), :] = jnp.concatenate(total, axis=0)

    def absolute(load):
        return jnp.concatenate(
            [
                jnp.concatenate(
                    [load(row, col).reshape(block_rows, block_cols, channels) for col in range(col_count)], axis=1
                )
                for row in range(row_count)
            ],
            axis=0,
        ).reshape(whole, channels)

    crossed = product[...].astype(jnp.bfloat16).astype(jnp.float32)
    mixed = layer_norm(crossed).astype(jnp.bfloat16)
    gate = absolute(lambda row, col: outgate[pl.ds(pl.multiple_of(starts[row][col], pairs), pairs), :])
    track = absolute(lambda row, col: crop_ref[slot_at(row, col), :pairs, :].astype(jnp.float32))
    summed = track + gate * dot(mixed, mult_outproj_ref[...])
    after[...] = summed
    again = layer_norm(summed)
    product[...] = again
    key_of_lane = lax.broadcasted_iota(jnp.int32, (length, spans), 1) % length
    on_key = (lax.broadcasted_iota(jnp.int32, (length, spans), 0) == key_of_lane).astype(jnp.float32)
    wide = dot(again.astype(jnp.bfloat16), bias_wide_ref[...]).astype(jnp.bfloat16).astype(jnp.float32)
    bias[...] = jnp.sum(wide.reshape(length, length, spans) * on_key[None], axis=1)

    own = pl.ds(pl.multiple_of(me * own_rows * length, own_rows * length), own_rows * length)
    residual = after[own, :]
    source = product[own, :].astype(jnp.bfloat16)
    projected = dot(source, attn_proj_ref[...])
    queries = (projected[:, :inner] * head_width ** (-0.5)).astype(jnp.bfloat16)
    keys = projected[:, inner : 2 * inner]
    values = projected[:, 2 * inner : 3 * inner]
    gating = sigmoid(projected[:, 3 * inner :])
    first_row = me * own_rows
    part = first_row // block_rows
    key_mask = jnp.zeros(key_lane.shape, jnp.float32)
    for col in range(col_count):
        mask = crop_ref[slot_at(part, col), pairs:, :]
        key_mask = key_mask + dot(mask, key_place_ref[col])
    key_lane[...] = key_mask
    head_of_lane = lax.broadcasted_iota(jnp.int32, (1, spans), 1) // length
    head_of_row = lax.broadcasted_iota(jnp.int32, (spans, inner), 0) // length
    head_of_channel = lax.broadcasted_iota(jnp.int32, (spans, inner), 1) // head_width
    same_head = (head_of_row == head_of_channel).astype(jnp.float32)
    gathered = []
    for row in range(own_rows):
        here = slice(row * length, (row + 1) * length)
        tall_keys = (jnp.concatenate([keys[here]] * heads, axis=0) * same_head).astype(jnp.bfloat16)
        tall_values = (jnp.concatenate([values[here]] * heads, axis=0) * same_head).astype(jnp.bfloat16)
        scores = lax.dot_general(
            queries[here], tall_keys, (((1,), (1,)), ((), ())), preferred_element_type=jnp.float32
        )
        allowed = key_lane[pl.ds(first_row - part * block_rows + row, 1), :] > 0.5
        scores = jnp.where(allowed, scores + bias[...], masked_score)
        top = jnp.zeros_like(scores)
        for head in range(heads):
            here_lanes = head_of_lane == head
            most = jnp.max(jnp.where(here_lanes, scores, -jnp.inf), axis=1, keepdims=True)
            top = jnp.where(here_lanes, most, top)
        expo = jnp.exp(scores - top)
        whole = jnp.zeros_like(scores)
        for head in range(heads):
            here_lanes = head_of_lane == head
            amount = jnp.sum(jnp.where(here_lanes, expo, 0.0), axis=1, keepdims=True)
            whole = jnp.where(here_lanes, amount, whole)
        gathered.append(dot((expo / whole).astype(jnp.bfloat16), tall_values))
    gated = (gating * jnp.concatenate(gathered, axis=0)).astype(jnp.bfloat16)
    residual = residual + dot(gated, attn_outproj_ref[...])
    source = layer_norm(residual).astype(jnp.bfloat16)
    gate = dot(source, trans_gate_ref[...])
    transit = (gate * sigmoid(gate) * dot(source, trans_value_ref[...])).astype(jnp.bfloat16)
    out_ref[...] = (residual + dot(transit, trans_outproj_ref[...])).astype(out_ref.dtype)


def gathered_crop(
    pair_track,
    pair_mask,
    token_mask,
    mult_gate,
    mult_value,
    mult_outgate,
    mult_outproj,
    attn_proj,
    attn_bias,
    attn_outproj,
    trans_gate,
    trans_value,
    trans_outproj,
):
    row_count, col_count = lax.axis_size("row"), lax.axis_size("col")
    devices = row_count * col_count
    block_rows, block_cols, channels = pair_track.shape
    length = block_cols * col_count
    pairs = block_rows * block_cols
    below = -(-block_rows // 16) * 16
    own_rows = length // devices
    heads = attn_bias.shape[1]
    spans = heads * length
    padded_mask = jnp.pad(pair_mask, ((pairs, below - block_rows), (0, channels - block_cols)))
    block = jnp.where(
        lax.broadcasted_iota(jnp.int32, (pairs + below, channels), 0) < pairs,
        jnp.pad(pair_track.reshape(pairs, channels), ((0, below), (0, 0))),
        jnp.where(padded_mask > 0, 1, 0).astype(pair_track.dtype),
    )
    crop = block[None]
    slots = [0]
    mask = devices // 2
    while mask:
        turn = mask | 1
        crop = jnp.concatenate(
            [crop, lax.ppermute(crop, crop_axes, [(i, i ^ turn) for i in range(devices)])]
        )
        slots = slots + [slot ^ turn for slot in slots]
        mask //= 2
    tokens = token_mask.astype(jnp.float32)
    token_pair = (
        tokens.reshape(row_count, 1, block_rows, 1) * tokens.reshape(1, col_count, 1, block_cols)
    ).reshape(devices, block_rows, block_cols)
    token_pair = jnp.pad(token_pair, ((0, 0), (0, 0), (0, lanes - block_cols)))
    key_place = (jnp.arange(lanes)[:, None] == jnp.arange(spans)[None, :] % block_cols)[None] & (
        jnp.arange(col_count)[:, None, None] == (jnp.arange(spans) % length // block_cols)[None, None, :]
    )
    key_place = key_place.astype(jnp.bfloat16) * jnp.tile(token_mask, heads).astype(jnp.bfloat16)
    bias_wide = jnp.repeat(attn_bias, length, axis=1)
    flat = pltpu.VMEM((length * length, channels), jnp.float32)
    out = pl.pallas_call(
        functools.partial(crop_kernel, tuple(slots), col_count),
        out_shape=jax.ShapeDtypeStruct((own_rows * length, channels), jnp.bfloat16),
        in_specs=[pl.BlockSpec(memory_space=pltpu.VMEM)] * 13,
        out_specs=pl.BlockSpec(memory_space=pltpu.VMEM),
        scratch_shapes=[flat] * 5
        + [pltpu.VMEM((length, spans), jnp.float32), pltpu.VMEM((below, spans), jnp.float32)],
        compiler_params=pltpu.CompilerParams(vmem_limit_bytes=48 << 20),
        name="crop",
    )(
        crop,
        token_pair,
        key_place,
        mult_gate,
        mult_value,
        mult_outgate,
        mult_outproj,
        attn_proj,
        bias_wide,
        attn_outproj,
        trans_gate,
        trans_value,
        trans_outproj,
    )
    return out.reshape(own_rows, length, channels)


def normalize(values, axis):
    widened = values.astype(jnp.float32)
    center = widened - jnp.mean(widened, axis=axis, keepdims=True)
    spread = jnp.mean(center * center, axis=axis, keepdims=True)
    return center * lax.rsqrt(spread + epsilon)


def project(normed, weight):
    return jnp.einsum("rkc,cd->rkd", normed, weight, preferred_element_type=jnp.float32)


def split_crop(
    pair_track,
    pair_mask,
    token_mask,
    mult_gate,
    mult_value,
    mult_outgate,
    mult_outproj,
    attn_proj,
    attn_bias,
    attn_outproj,
    trans_gate,
    trans_value,
    trans_outproj,
):
    col_count = lax.axis_size("col")
    rows_here = pair_track.shape[0] // col_count
    full_rows, full_mask = (
        lax.all_to_all(pair_track, "col", split_axis=0, concat_axis=1, tiled=True),
        lax.all_to_all(
            pair_mask.astype(jnp.bfloat16), "col", split_axis=0, concat_axis=1, tiled=True
        ),
    )
    length = full_rows.shape[1]
    row_start = (lax.axis_index("row") * col_count + lax.axis_index("col")) * rows_here
    token_rows = token_mask.astype(jnp.float32)
    own_tokens = lax.dynamic_slice_in_dim(token_rows, row_start, rows_here, 0)
    key_mask = full_mask.astype(jnp.float32) * token_rows[None, :]
    mult_mask = key_mask * own_tokens[:, None]
    residual = full_rows.astype(jnp.float32)
    normed = normalize(full_rows, 2).astype(jnp.bfloat16)
    gate_logit = jnp.einsum("rkc,cd->drk", normed, mult_gate, preferred_element_type=jnp.float32)
    value_part = jnp.einsum("rkc,cd->drk", normed, mult_value, preferred_element_type=jnp.float32)
    hidden = mult_gate.shape[1] // 2
    paired = (jax.nn.sigmoid(gate_logit) * value_part * mult_mask[None]).astype(jnp.bfloat16)
    paired = paired.reshape(2, hidden, rows_here, length)
    spread_pair = lax.all_to_all(paired, "col", split_axis=1, concat_axis=2, tiled=True)
    left_side = spread_pair[0]
    crossed = jnp.einsum(
        "cik,cjk->cij",
        left_side,
        lax.all_gather(spread_pair[1], "row", axis=1, tiled=True),
        preferred_element_type=jnp.float32,
    )
    crossed = crossed.astype(jnp.bfloat16)
    merged = lax.all_to_all(crossed, "col", split_axis=1, concat_axis=0, tiled=True)
    mixed_norm = normalize(merged, 0).astype(jnp.bfloat16)
    update = jnp.einsum("crk,cd->rkd", mixed_norm, mult_outproj, preferred_element_type=jnp.float32)
    outgate = jax.nn.sigmoid(project(normed, mult_outgate))
    residual = residual + outgate * update
    normed = normalize(residual, 2).astype(jnp.bfloat16)
    head_count = attn_bias.shape[1]
    inner_width = attn_outproj.shape[0]
    head_width = inner_width // head_count
    projected = project(normed, attn_proj)
    queries = (projected[:, :, :inner_width] * head_width ** (-0.5)).astype(jnp.bfloat16)
    queries = queries.reshape(rows_here, length, head_count, head_width)
    key_rows = (
        projected[:, :, inner_width : 2 * inner_width]
        .astype(jnp.bfloat16)
        .reshape(rows_here, length, head_count, head_width)
    )
    value_rows = (
        projected[:, :, 2 * inner_width : 3 * inner_width]
        .astype(jnp.bfloat16)
        .reshape(rows_here, length, head_count, head_width)
    )
    gating = jax.nn.sigmoid(projected[:, :, 3 * inner_width :])
    bias_local = jnp.einsum(
        "rkc,ch->hrk", normed, attn_bias, preferred_element_type=jnp.float32
    ).astype(jnp.bfloat16)
    allowed = key_mask > 0.5
    segment = lax.all_gather(bias_local, ("row", "col"), axis=1, tiled=True)
    amount = segment.shape[1]
    scores = jnp.einsum("rjhd,rkhd->hrjk", queries, key_rows, preferred_element_type=jnp.float32)
    scores = scores + segment.astype(jnp.float32)[:, None]
    scores = jnp.where(allowed[None, :, None, :], scores, masked_score)
    row_max = jnp.max(scores, axis=3, keepdims=True)
    expo = jnp.exp(scores - row_max)
    attn_weights = (expo / jnp.sum(expo, axis=3, keepdims=True)).astype(jnp.bfloat16)
    mixed_heads = jnp.einsum(
        "hrjk,rkhd->rjhd", attn_weights, value_rows, preferred_element_type=jnp.float32
    )
    gated_out = (gating * mixed_heads.reshape(rows_here, amount, inner_width)).astype(jnp.bfloat16)
    attended = jnp.einsum(
        "rjd,dc->rjc", gated_out, attn_outproj, preferred_element_type=jnp.float32
    )
    residual = residual + attended
    normed = normalize(residual, 2).astype(jnp.bfloat16)
    transit = (jax.nn.silu(project(normed, trans_gate)) * project(normed, trans_value)).astype(
        jnp.bfloat16
    )
    residual = residual + project(transit, trans_outproj)
    return residual.astype(jnp.bfloat16)


def on_device(pair_track, *others):
    devices = lax.axis_size("row") * lax.axis_size("col")
    pairs = pair_track.shape[0] * pair_track.shape[1] * devices
    heads = others[7].shape[1]
    length = pair_track.shape[1] * lax.axis_size("col")
    fits = pairs * pair_track.shape[2] * 4 <= crop_bytes_max
    if fits and heads * length == lanes and pair_track.shape[2] == lanes and devices & (devices - 1) == 0:
        return gathered_crop(pair_track, *others)
    return split_crop(pair_track, *others)


def solution(mesh):
    return jax.shard_map(
        on_device,
        mesh=mesh,
        in_specs=(
            P(("grp", "row"), "col", None),
            P(("grp", "row"), "col"),
            P("grp"),
            P(),
            P(),
            P(),
            P(),
            P(),
            P(),
            P(),
            P(),
            P(),
            P(),
        ),
        out_specs=P(("grp", "row", "col"), None, None),
        check_vma=False,
    )
```

```python
import functools

import jax
import jax.numpy as jnp
from jax import lax
from jax.experimental import pallas as pl
from jax.experimental.pallas import tpu as pltpu
from jax.sharding import PartitionSpec as P

epsilon = 1e-05
masked_score = -1000000000.0
crop_axes = ("row", "col")
lanes = 128
crop_bytes_max = 1 << 20


def dot(left, right):
    return jnp.dot(left, right, preferred_element_type=jnp.float32)


def sigmoid(values):
    return 1.0 / (1.0 + jnp.exp(-values))


def layer_norm(values):
    center = values - jnp.mean(values, axis=-1, keepdims=True)
    spread = jnp.mean(center * center, axis=-1, keepdims=True)
    return center * lax.rsqrt(spread + epsilon)


def slot_index(offset, devices):
    top = devices.bit_length() - 2
    slot = offset & 1
    for bit in range(1, top + 1):
        slot = slot ^ ((offset >> bit) & 1)
    slot = slot << top
    for bit in range(1, top + 1):
        slot = slot | (((offset >> bit) & 1) << (top - bit))
    return slot


def crop_kernel(
    slots,
    col_count,
    here_ref,
    there_ref,
    token_pair_ref,
    key_place_ref,
    mult_gate_ref,
    mult_value_ref,
    mult_outgate_ref,
    mult_outproj_ref,
    attn_proj_ref,
    bias_wide_ref,
    attn_outproj_ref,
    trans_gate_ref,
    trans_value_ref,
    trans_outproj_ref,
    out_ref,
    crop_ref,
    left,
    right,
    outgate,
    product,
    after,
    bias,
    key_lane,
):
    channels = after.shape[1]
    hidden = mult_outproj_ref.shape[0]
    inner = attn_outproj_ref.shape[0]
    length, spans = bias.shape
    heads = spans // length
    head_width = inner // heads
    own_rows = out_ref.shape[0] // length
    devices = len(slots)
    row_count = devices // col_count
    block_rows, block_cols = length // row_count, length // col_count
    pairs = block_rows * block_cols
    whole = length * length
    me = lax.axis_index(crop_axes)

    def slot_at(row, col):
        return slot_index((row * col_count + col) ^ me, devices)

    crop_ref[: devices // 2] = here_ref[...]
    crop_ref[devices // 2 :] = there_ref[...]
    packed = jnp.concatenate([here_ref[:, :pairs, :], there_ref[:, :pairs, :]], axis=0).reshape(whole, channels)
    source = layer_norm(packed.astype(jnp.float32)).astype(jnp.bfloat16)
    diagonal = (
        lax.broadcasted_iota(jnp.int32, (block_cols, lanes), 0)
        == lax.broadcasted_iota(jnp.int32, (block_cols, lanes), 1)
    ).astype(jnp.float32)
    masks = []
    for slot, offset in enumerate(slots):
        half_ref = (here_ref, there_ref)[slot // (devices // 2)]
        mask = half_ref[slot % (devices // 2), pairs:, :].astype(jnp.float32)[:block_rows] * token_pair_ref[me ^ offset]
        masks.append((mask[:, None, :] * diagonal[None]).reshape(pairs, lanes))
    mask = dot(jnp.concatenate(masks, axis=0).astype(jnp.bfloat16), jnp.ones((lanes, channels), jnp.bfloat16))
    outgate[...] = sigmoid(dot(source, mult_outgate_ref[...]))
    paired = sigmoid(dot(source, mult_gate_ref[...])) * dot(source, mult_value_ref[...])
    left[...] = (paired[:, :hidden] * mask).astype(jnp.bfloat16).astype(jnp.float32)
    turned = (paired[:, hidden:] * mask).astype(jnp.bfloat16).astype(jnp.float32)
    for slot in range(devices):
        for row in range(block_rows):
            start = slot * pairs + row * block_cols
            right[pl.ds(slot * pairs + row, block_cols, stride=block_rows), :] = turned[start : start + block_cols]

    starts = [[slot_at(row, col) * pairs for col in range(col_count)] for row in range(row_count)]

    @pl.loop(0, row_count)
    def _(part):
        total = [jnp.zeros((length, hidden), jnp.float32) for _ in range(block_rows)]
        for col in range(col_count):
            start = slot_at(part, col) * pairs
            for k in range(block_cols):
                column = jnp.concatenate(
                    [
                        right[pl.ds(pl.multiple_of(starts[row][col] + k * block_rows, block_rows), block_rows), :]
                        for row in range(row_count)
                    ],
                    axis=0,
                )
                for row in range(block_rows):
                    total[row] = total[row] + left[pl.ds(start + row * block_cols + k, 1), :] * column
        step = block_rows * length
        product[pl.ds(pl.multiple_of(part * step, step), step), :] = jnp.concatenate(total, axis=0)

    def absolute(load):
        return jnp.concatenate(
            [
                jnp.concatenate(
                    [load(row, col).reshape(block_rows, block_cols, channels) for col in range(col_count)], axis=1
                )
                for row in range(row_count)
            ],
            axis=0,
        ).reshape(whole, channels)

    crossed = product[...].astype(jnp.bfloat16).astype(jnp.float32)
    mixed = layer_norm(crossed).astype(jnp.bfloat16)
    gate = absolute(lambda row, col: outgate[pl.ds(pl.multiple_of(starts[row][col], pairs), pairs), :])
    track = absolute(lambda row, col: crop_ref[slot_at(row, col), :pairs, :].astype(jnp.float32))
    summed = track + gate * dot(mixed, mult_outproj_ref[...])
    after[...] = summed
    again = layer_norm(summed)
    product[...] = again
    key_of_lane = lax.broadcasted_iota(jnp.int32, (length, spans), 1) % length
    on_key = (lax.broadcasted_iota(jnp.int32, (length, spans), 0) == key_of_lane).astype(jnp.float32)
    wide = dot(again.astype(jnp.bfloat16), bias_wide_ref[...]).astype(jnp.bfloat16).astype(jnp.float32)
    bias[...] = jnp.sum(wide.reshape(length, length, spans) * on_key[None], axis=1)

    own = pl.ds(pl.multiple_of(me * own_rows * length, own_rows * length), own_rows * length)
    residual = after[own, :]
    source = product[own, :].astype(jnp.bfloat16)
    projected = dot(source, attn_proj_ref[...])
    queries = (projected[:, :inner] * head_width ** (-0.5)).astype(jnp.bfloat16)
    keys = projected[:, inner : 2 * inner]
    values = projected[:, 2 * inner : 3 * inner]
    gating = sigmoid(projected[:, 3 * inner :])
    first_row = me * own_rows
    part = first_row // block_rows
    key_mask = jnp.zeros(key_lane.shape, jnp.float32)
    for col in range(col_count):
        mask = crop_ref[slot_at(part, col), pairs:, :]
        key_mask = key_mask + dot(mask, key_place_ref[col])
    key_lane[...] = key_mask
    head_of_lane = lax.broadcasted_iota(jnp.int32, (1, spans), 1) // length
    head_of_row = lax.broadcasted_iota(jnp.int32, (spans, inner), 0) // length
    head_of_channel = lax.broadcasted_iota(jnp.int32, (spans, inner), 1) // head_width
    same_head = (head_of_row == head_of_channel).astype(jnp.float32)
    gathered = []
    for row in range(own_rows):
        here = slice(row * length, (row + 1) * length)
        tall_keys = (jnp.concatenate([keys[here]] * heads, axis=0) * same_head).astype(jnp.bfloat16)
        tall_values = (jnp.concatenate([values[here]] * heads, axis=0) * same_head).astype(jnp.bfloat16)
        scores = lax.dot_general(
            queries[here], tall_keys, (((1,), (1,)), ((), ())), preferred_element_type=jnp.float32
        )
        allowed = key_lane[pl.ds(first_row - part * block_rows + row, 1), :] > 0.5
        scores = jnp.where(allowed, scores + bias[...], masked_score)
        top = jnp.zeros_like(scores)
        for head in range(heads):
            here_lanes = head_of_lane == head
            most = jnp.max(jnp.where(here_lanes, scores, -jnp.inf), axis=1, keepdims=True)
            top = jnp.where(here_lanes, most, top)
        expo = jnp.exp(scores - top)
        whole = jnp.zeros_like(scores)
        for head in range(heads):
            here_lanes = head_of_lane == head
            amount = jnp.sum(jnp.where(here_lanes, expo, 0.0), axis=1, keepdims=True)
            whole = jnp.where(here_lanes, amount, whole)
        gathered.append(dot((expo / whole).astype(jnp.bfloat16), tall_values))
    gated = (gating * jnp.concatenate(gathered, axis=0)).astype(jnp.bfloat16)
    residual = residual + dot(gated, attn_outproj_ref[...])
    source = layer_norm(residual).astype(jnp.bfloat16)
    gate = dot(source, trans_gate_ref[...])
    transit = (gate * sigmoid(gate) * dot(source, trans_value_ref[...])).astype(jnp.bfloat16)
    out_ref[...] = (residual + dot(transit, trans_outproj_ref[...])).astype(out_ref.dtype)


def gathered_crop(
    pair_track,
    pair_mask,
    token_mask,
    mult_gate,
    mult_value,
    mult_outgate,
    mult_outproj,
    attn_proj,
    attn_bias,
    attn_outproj,
    trans_gate,
    trans_value,
    trans_outproj,
):
    row_count, col_count = lax.axis_size("row"), lax.axis_size("col")
    devices = row_count * col_count
    block_rows, block_cols, channels = pair_track.shape
    length = block_cols * col_count
    pairs = block_rows * block_cols
    below = -(-block_rows // 16) * 16
    own_rows = length // devices
    heads = attn_bias.shape[1]
    spans = heads * length
    padded_mask = jnp.pad(pair_mask, ((pairs, below - block_rows), (0, channels - block_cols)))
    block = jnp.where(
        lax.broadcasted_iota(jnp.int32, (pairs + below, channels), 0) < pairs,
        jnp.pad(pair_track.reshape(pairs, channels), ((0, below), (0, 0))),
        jnp.where(padded_mask > 0, 1, 0).astype(pair_track.dtype),
    )
    crop = block[None]
    slots = [0]
    mask = devices // 2
    while mask:
        turn = mask | 1
        pairing = [(i, i ^ turn) for i in range(devices)]
        parts = 2 if mask > 1 and crop.shape[0] > 2 else 1
        arrived = [lax.ppermute(part, crop_axes, pairing) for part in jnp.split(crop, parts)]
        halves = crop, arrived[0]
        crop = jnp.concatenate([crop] + arrived)
        slots = slots + [slot ^ turn for slot in slots]
        mask //= 2
    tokens = token_mask.astype(jnp.float32)
    token_pair = (
        tokens.reshape(row_count, 1, block_rows, 1) * tokens.reshape(1, col_count, 1, block_cols)
    ).reshape(devices, block_rows, block_cols)
    token_pair = jnp.pad(token_pair, ((0, 0), (0, 0), (0, lanes - block_cols)))
    key_place = (jnp.arange(lanes)[:, None] == jnp.arange(spans)[None, :] % block_cols)[None] & (
        jnp.arange(col_count)[:, None, None] == (jnp.arange(spans) % length // block_cols)[None, None, :]
    )
    key_place = key_place.astype(jnp.bfloat16) * jnp.tile(token_mask, heads).astype(jnp.bfloat16)
    bias_wide = jnp.repeat(attn_bias, length, axis=1)
    flat = pltpu.VMEM((length * length, channels), jnp.float32)
    out = pl.pallas_call(
        functools.partial(crop_kernel, tuple(slots), col_count),
        out_shape=jax.ShapeDtypeStruct((own_rows * length, channels), jnp.bfloat16),
        in_specs=[pl.BlockSpec(memory_space=pltpu.VMEM)] * 14,
        out_specs=pl.BlockSpec(memory_space=pltpu.VMEM),
        scratch_shapes=[pltpu.VMEM((devices,) + halves[0].shape[1:], halves[0].dtype)]
        + [flat] * 5
        + [pltpu.VMEM((length, spans), jnp.float32), pltpu.VMEM((below, spans), jnp.float32)],
        compiler_params=pltpu.CompilerParams(vmem_limit_bytes=48 << 20),
        name="crop",
    )(
        *halves,
        token_pair,
        key_place,
        mult_gate,
        mult_value,
        mult_outgate,
        mult_outproj,
        attn_proj,
        bias_wide,
        attn_outproj,
        trans_gate,
        trans_value,
        trans_outproj,
    )
    return out.reshape(own_rows, length, channels)


def normalize(values, axis):
    widened = values.astype(jnp.float32)
    center = widened - jnp.mean(widened, axis=axis, keepdims=True)
    spread = jnp.mean(center * center, axis=axis, keepdims=True)
    return center * lax.rsqrt(spread + epsilon)


def project(normed, weight):
    return jnp.einsum("rkc,cd->rkd", normed, weight, preferred_element_type=jnp.float32)


def split_crop(
    pair_track,
    pair_mask,
    token_mask,
    mult_gate,
    mult_value,
    mult_outgate,
    mult_outproj,
    attn_proj,
    attn_bias,
    attn_outproj,
    trans_gate,
    trans_value,
    trans_outproj,
):
    col_count = lax.axis_size("col")
    rows_here = pair_track.shape[0] // col_count
    full_rows, full_mask = (
        lax.all_to_all(pair_track, "col", split_axis=0, concat_axis=1, tiled=True),
        lax.all_to_all(
            pair_mask.astype(jnp.bfloat16), "col", split_axis=0, concat_axis=1, tiled=True
        ),
    )
    length = full_rows.shape[1]
    row_start = (lax.axis_index("row") * col_count + lax.axis_index("col")) * rows_here
    token_rows = token_mask.astype(jnp.float32)
    own_tokens = lax.dynamic_slice_in_dim(token_rows, row_start, rows_here, 0)
    key_mask = full_mask.astype(jnp.float32) * token_rows[None, :]
    mult_mask = key_mask * own_tokens[:, None]
    residual = full_rows.astype(jnp.float32)
    normed = normalize(full_rows, 2).astype(jnp.bfloat16)
    gate_logit = jnp.einsum("rkc,cd->drk", normed, mult_gate, preferred_element_type=jnp.float32)
    value_part = jnp.einsum("rkc,cd->drk", normed, mult_value, preferred_element_type=jnp.float32)
    hidden = mult_gate.shape[1] // 2
    paired = (jax.nn.sigmoid(gate_logit) * value_part * mult_mask[None]).astype(jnp.bfloat16)
    paired = paired.reshape(2, hidden, rows_here, length)
    spread_pair = lax.all_to_all(paired, "col", split_axis=1, concat_axis=2, tiled=True)
    left_side = spread_pair[0]
    crossed = jnp.einsum(
        "cik,cjk->cij",
        left_side,
        lax.all_gather(spread_pair[1], "row", axis=1, tiled=True),
        preferred_element_type=jnp.float32,
    )
    crossed = crossed.astype(jnp.bfloat16)
    merged = lax.all_to_all(crossed, "col", split_axis=1, concat_axis=0, tiled=True)
    mixed_norm = normalize(merged, 0).astype(jnp.bfloat16)
    update = jnp.einsum("crk,cd->rkd", mixed_norm, mult_outproj, preferred_element_type=jnp.float32)
    outgate = jax.nn.sigmoid(project(normed, mult_outgate))
    residual = residual + outgate * update
    normed = normalize(residual, 2).astype(jnp.bfloat16)
    head_count = attn_bias.shape[1]
    inner_width = attn_outproj.shape[0]
    head_width = inner_width // head_count
    projected = project(normed, attn_proj)
    queries = (projected[:, :, :inner_width] * head_width ** (-0.5)).astype(jnp.bfloat16)
    queries = queries.reshape(rows_here, length, head_count, head_width)
    key_rows = (
        projected[:, :, inner_width : 2 * inner_width]
        .astype(jnp.bfloat16)
        .reshape(rows_here, length, head_count, head_width)
    )
    value_rows = (
        projected[:, :, 2 * inner_width : 3 * inner_width]
        .astype(jnp.bfloat16)
        .reshape(rows_here, length, head_count, head_width)
    )
    gating = jax.nn.sigmoid(projected[:, :, 3 * inner_width :])
    bias_local = jnp.einsum(
        "rkc,ch->hrk", normed, attn_bias, preferred_element_type=jnp.float32
    ).astype(jnp.bfloat16)
    allowed = key_mask > 0.5
    segment = lax.all_gather(bias_local, ("row", "col"), axis=1, tiled=True)
    amount = segment.shape[1]
    scores = jnp.einsum("rjhd,rkhd->hrjk", queries, key_rows, preferred_element_type=jnp.float32)
    scores = scores + segment.astype(jnp.float32)[:, None]
    scores = jnp.where(allowed[None, :, None, :], scores, masked_score)
    row_max = jnp.max(scores, axis=3, keepdims=True)
    expo = jnp.exp(scores - row_max)
    attn_weights = (expo / jnp.sum(expo, axis=3, keepdims=True)).astype(jnp.bfloat16)
    mixed_heads = jnp.einsum(
        "hrjk,rkhd->rjhd", attn_weights, value_rows, preferred_element_type=jnp.float32
    )
    gated_out = (gating * mixed_heads.reshape(rows_here, amount, inner_width)).astype(jnp.bfloat16)
    attended = jnp.einsum(
        "rjd,dc->rjc", gated_out, attn_outproj, preferred_element_type=jnp.float32
    )
    residual = residual + attended
    normed = normalize(residual, 2).astype(jnp.bfloat16)
    transit = (jax.nn.silu(project(normed, trans_gate)) * project(normed, trans_value)).astype(
        jnp.bfloat16
    )
    residual = residual + project(transit, trans_outproj)
    return residual.astype(jnp.bfloat16)


def on_device(pair_track, *others):
    devices = lax.axis_size("row") * lax.axis_size("col")
    pairs = pair_track.shape[0] * pair_track.shape[1] * devices
    heads = others[7].shape[1]
    length = pair_track.shape[1] * lax.axis_size("col")
    fits = pairs * pair_track.shape[2] * 4 <= crop_bytes_max
    if fits and heads * length == lanes and pair_track.shape[2] == lanes and devices & (devices - 1) == 0:
        return gathered_crop(pair_track, *others)
    return split_crop(pair_track, *others)


def solution(mesh):
    return jax.shard_map(
        on_device,
        mesh=mesh,
        in_specs=(
            P(("grp", "row"), "col", None),
            P(("grp", "row"), "col"),
            P("grp"),
            P(),
            P(),
            P(),
            P(),
            P(),
            P(),
            P(),
            P(),
            P(),
            P(),
        ),
        out_specs=P(("grp", "row", "col"), None, None),
        check_vma=False,
    )
```

```python
import functools

import jax
import jax.numpy as jnp
from jax import lax
from jax.experimental import pallas as pl
from jax.experimental.pallas import tpu as pltpu
from jax.sharding import PartitionSpec as P

epsilon = 1e-05
masked_score = -1000000000.0
crop_axes = ("row", "col")
lanes = 128
crop_bytes_max = 1 << 20


def dot(left, right):
    return jnp.dot(left, right, preferred_element_type=jnp.float32)


def sigmoid(values):
    return 0.5 * jnp.tanh(0.5 * values) + 0.5


def layer_norm(values):
    center = values - jnp.mean(values, axis=-1, keepdims=True)
    spread = jnp.mean(center * center, axis=-1, keepdims=True)
    return center * lax.rsqrt(spread + epsilon)


def slot_index(offset, devices):
    top = devices.bit_length() - 2
    slot = offset & 1
    for bit in range(1, top + 1):
        slot = slot ^ ((offset >> bit) & 1)
    slot = slot << top
    for bit in range(1, top + 1):
        slot = slot | (((offset >> bit) & 1) << (top - bit))
    return slot


def crop_kernel(
    slots,
    col_count,
    here_ref,
    there_ref,
    token_pair_ref,
    key_place_ref,
    mult_gate_ref,
    mult_value_ref,
    mult_outgate_ref,
    mult_outproj_ref,
    attn_proj_ref,
    attn_bias_ref,
    attn_outproj_ref,
    trans_gate_ref,
    trans_value_ref,
    trans_outproj_ref,
    out_ref,
    crop_ref,
    left,
    right,
    outgate,
    product,
    bias,
    key_lane,
    bias_wide_ref,
):
    channels = outgate.shape[1]
    hidden = mult_outproj_ref.shape[0]
    inner = attn_outproj_ref.shape[0]
    length, spans = bias.shape
    heads = attn_bias_ref.shape[0]
    head_width = inner // heads
    own_rows = out_ref.shape[0] // length
    devices = len(slots)
    row_count = devices // col_count
    block_rows, block_cols = length // row_count, length // col_count
    pairs = block_rows * block_cols
    whole = length * length
    me = lax.axis_index(crop_axes)

    def slot_at(row, col):
        return slot_index((row * col_count + col) ^ me, devices)

    crop_ref[: devices // 2] = here_ref[...]
    crop_ref[devices // 2 :] = there_ref[...]
    packed = jnp.concatenate([here_ref[:, :pairs, :], there_ref[:, :pairs, :]], axis=0).reshape(whole, channels)
    source = layer_norm(packed.astype(jnp.float32)).astype(jnp.bfloat16)
    diagonal = (
        lax.broadcasted_iota(jnp.int32, (block_cols, lanes), 0)
        == lax.broadcasted_iota(jnp.int32, (block_cols, lanes), 1)
    ).astype(jnp.float32)
    head_lanes = (
        lax.broadcasted_iota(jnp.int32, (heads, spans), 0)
        == lax.broadcasted_iota(jnp.int32, (heads, spans), 1) // length
    ).astype(jnp.float32)
    bias_wide_ref[...] = lax.dot_general(
        attn_bias_ref[...].astype(jnp.float32),
        head_lanes,
        (((0,), (0,)), ((), ())),
        preferred_element_type=jnp.float32,
    ).astype(jnp.bfloat16)
    masks = []
    for slot, offset in enumerate(slots):
        half_ref = (here_ref, there_ref)[slot // (devices // 2)]
        mask = half_ref[slot % (devices // 2), pairs:, :].astype(jnp.float32)[:block_rows] * token_pair_ref[me ^ offset]
        masks.append((mask[:, None, :] * diagonal[None]).reshape(pairs, lanes))
    mask = dot(jnp.concatenate(masks, axis=0).astype(jnp.bfloat16), jnp.ones((lanes, channels), jnp.bfloat16))
    outgate[...] = sigmoid(dot(source, mult_outgate_ref[...]))
    paired = sigmoid(dot(source, mult_gate_ref[...])) * dot(source, mult_value_ref[...])
    left[...] = (paired[:, :hidden] * mask).astype(jnp.bfloat16).astype(jnp.float32)
    turned = (paired[:, hidden:] * mask).astype(jnp.bfloat16).astype(jnp.float32)
    for slot in range(devices):
        for row in range(block_rows):
            start = slot * pairs + row * block_cols
            right[pl.ds(slot * pairs + row, block_cols, stride=block_rows), :] = turned[start : start + block_cols]

    starts = [[slot_at(row, col) * pairs for col in range(col_count)] for row in range(row_count)]

    for part in range(row_count):
        total = [jnp.zeros((length, hidden), jnp.float32) for _ in range(block_rows)]
        for col in range(col_count):
            start = starts[part][col]
            for k in range(block_cols):
                column = jnp.concatenate(
                    [
                        right[pl.ds(pl.multiple_of(starts[row][col] + k * block_rows, block_rows), block_rows), :]
                        for row in range(row_count)
                    ],
                    axis=0,
                )
                for row in range(block_rows):
                    total[row] = total[row] + left[pl.ds(start + row * block_cols + k, 1), :] * column
        step = block_rows * length
        product[pl.ds(pl.multiple_of(part * step, step), step), :] = jnp.concatenate(total, axis=0)

    def absolute(load):
        return jnp.concatenate(
            [
                jnp.concatenate(
                    [load(row, col).reshape(block_rows, block_cols, channels) for col in range(col_count)], axis=1
                )
                for row in range(row_count)
            ],
            axis=0,
        ).reshape(whole, channels)

    def grown(rows, track, gate):
        mixed = layer_norm(rows.astype(jnp.bfloat16).astype(jnp.float32)).astype(jnp.bfloat16)
        rows = track + gate * dot(mixed, mult_outproj_ref[...])
        return rows, layer_norm(rows).astype(jnp.bfloat16)

    first_row = me * own_rows
    part = first_row // block_rows
    first_own = first_row - part * block_rows
    own_pairs = own_rows * block_cols
    inside = pl.ds(pl.multiple_of(first_own * block_cols, own_pairs), own_pairs)
    own_slots = [slot_at(part, col) for col in range(col_count)]

    def own_block(values):
        values = [value.reshape(own_rows, block_cols, channels) for value in values]
        return jnp.concatenate(values, axis=1).reshape(own_rows * length, channels)

    residual, source = grown(
        product[pl.ds(pl.multiple_of(me * own_rows * length, own_rows * length), own_rows * length), :],
        own_block([crop_ref[slot, inside, :].astype(jnp.float32) for slot in own_slots]),
        own_block(
            [
                outgate[pl.ds(pl.multiple_of(slot * pairs + first_own * block_cols, own_pairs), own_pairs), :]
                for slot in own_slots
            ]
        ),
    )
    projected = dot(source, attn_proj_ref[...])
    queries = (projected[:, :inner] * head_width ** (-0.5)).astype(jnp.bfloat16)
    keys = projected[:, inner : 2 * inner]
    values = projected[:, 2 * inner : 3 * inner]
    gating = sigmoid(projected[:, 3 * inner :])
    key_mask = jnp.zeros(key_lane.shape, jnp.float32)
    for col in range(col_count):
        mask = crop_ref[own_slots[col], pairs:, :]
        key_mask = key_mask + dot(mask, key_place_ref[col])
    key_lane[...] = key_mask
    head_of_lane = lax.broadcasted_iota(jnp.int32, (1, spans), 1) // length
    head_of_row = lax.broadcasted_iota(jnp.int32, (spans, inner), 0) // length
    head_of_channel = lax.broadcasted_iota(jnp.int32, (spans, inner), 1) // head_width
    same_head = (head_of_row == head_of_channel).astype(jnp.float32)
    _, again = grown(
        product[...],
        absolute(lambda row, col: crop_ref[slot_at(row, col), :pairs, :].astype(jnp.float32)),
        absolute(lambda row, col: outgate[pl.ds(pl.multiple_of(starts[row][col], pairs), pairs), :]),
    )
    key_of_lane = lax.broadcasted_iota(jnp.int32, (length, spans), 1) % length
    on_key = (lax.broadcasted_iota(jnp.int32, (length, spans), 0) == key_of_lane).astype(jnp.float32)
    wide = dot(again, bias_wide_ref[...]).astype(jnp.bfloat16).astype(jnp.float32)
    bias[...] = jnp.sum(wide.reshape(length, length, spans) * on_key[None], axis=1)

    gathered = []
    for row in range(own_rows):
        here = slice(row * length, (row + 1) * length)
        tall_keys = (jnp.concatenate([keys[here]] * heads, axis=0) * same_head).astype(jnp.bfloat16)
        tall_values = (jnp.concatenate([values[here]] * heads, axis=0) * same_head).astype(jnp.bfloat16)
        scores = lax.dot_general(
            queries[here], tall_keys, (((1,), (1,)), ((), ())), preferred_element_type=jnp.float32
        )
        allowed = key_lane[pl.ds(first_own + row, 1), :] > 0.5
        scores = jnp.where(allowed, scores + bias[...], masked_score)
        top = jnp.zeros_like(scores)
        for head in range(heads):
            here_lanes = head_of_lane == head
            most = jnp.max(jnp.where(here_lanes, scores, -jnp.inf), axis=1, keepdims=True)
            top = jnp.where(here_lanes, most, top)
        expo = jnp.exp(scores - top)
        whole = jnp.zeros_like(scores)
        for head in range(heads):
            here_lanes = head_of_lane == head
            amount = jnp.sum(jnp.where(here_lanes, expo, 0.0), axis=1, keepdims=True)
            whole = jnp.where(here_lanes, amount, whole)
        gathered.append(dot((expo / whole).astype(jnp.bfloat16), tall_values))
    gated = (gating * jnp.concatenate(gathered, axis=0)).astype(jnp.bfloat16)
    residual = residual + dot(gated, attn_outproj_ref[...])
    source = layer_norm(residual).astype(jnp.bfloat16)
    gate = dot(source, trans_gate_ref[...])
    transit = (gate * sigmoid(gate) * dot(source, trans_value_ref[...])).astype(jnp.bfloat16)
    out_ref[...] = (residual + dot(transit, trans_outproj_ref[...])).astype(out_ref.dtype)


def gathered_crop(
    pair_track,
    pair_mask,
    token_mask,
    mult_gate,
    mult_value,
    mult_outgate,
    mult_outproj,
    attn_proj,
    attn_bias,
    attn_outproj,
    trans_gate,
    trans_value,
    trans_outproj,
):
    row_count, col_count = lax.axis_size("row"), lax.axis_size("col")
    devices = row_count * col_count
    block_rows, block_cols, channels = pair_track.shape
    length = block_cols * col_count
    pairs = block_rows * block_cols
    below = -(-block_rows // 16) * 16
    own_rows = length // devices
    heads = attn_bias.shape[1]
    spans = heads * length
    padded_mask = jnp.pad(pair_mask, ((pairs, below - block_rows), (0, channels - block_cols)))
    block = jnp.where(
        lax.broadcasted_iota(jnp.int32, (pairs + below, channels), 0) < pairs,
        jnp.pad(pair_track.reshape(pairs, channels), ((0, below), (0, 0))),
        jnp.where(padded_mask > 0, 1, 0).astype(pair_track.dtype),
    )
    crop = block[None]
    slots = [0]
    mask = devices // 2
    while mask:
        turn = mask | 1
        pairing = [(i, i ^ turn) for i in range(devices)]
        parts = 2 if mask > 1 and crop.shape[0] > 2 else 1
        arrived = [lax.ppermute(part, crop_axes, pairing) for part in jnp.split(crop, parts)]
        halves = crop, arrived[0]
        crop = jnp.concatenate([crop] + arrived)
        slots = slots + [slot ^ turn for slot in slots]
        mask //= 2
    tokens = token_mask.astype(jnp.float32)
    token_pair = (
        tokens.reshape(row_count, 1, block_rows, 1) * tokens.reshape(1, col_count, 1, block_cols)
    ).reshape(devices, block_rows, block_cols)
    token_pair = jnp.pad(token_pair, ((0, 0), (0, 0), (0, lanes - block_cols)))
    key_place = (jnp.arange(lanes)[:, None] == jnp.arange(spans)[None, :] % block_cols)[None] & (
        jnp.arange(col_count)[:, None, None] == (jnp.arange(spans) % length // block_cols)[None, None, :]
    )
    key_place = key_place.astype(jnp.bfloat16) * jnp.tile(token_mask, heads).astype(jnp.bfloat16)
    flat = pltpu.VMEM((length * length, channels), jnp.float32)
    tall = pltpu.VMEM((length * length + pairs, channels), jnp.float32)
    out = pl.pallas_call(
        functools.partial(crop_kernel, tuple(slots), col_count),
        out_shape=jax.ShapeDtypeStruct((own_rows * length, channels), jnp.bfloat16),
        in_specs=[pl.BlockSpec(memory_space=pltpu.VMEM)] * 14,
        out_specs=pl.BlockSpec(memory_space=pltpu.VMEM),
        scratch_shapes=[pltpu.VMEM((devices,) + halves[0].shape[1:], halves[0].dtype)]
        + [flat, tall, flat, flat]
        + [pltpu.VMEM((length, spans), jnp.float32), pltpu.VMEM((below, spans), jnp.float32)]
        + [pltpu.VMEM((channels, spans), jnp.bfloat16)],
        compiler_params=pltpu.CompilerParams(vmem_limit_bytes=48 << 20),
        name="crop",
    )(
        *halves,
        token_pair,
        key_place,
        mult_gate,
        mult_value,
        mult_outgate,
        mult_outproj,
        attn_proj,
        attn_bias.T,
        attn_outproj,
        trans_gate,
        trans_value,
        trans_outproj,
    )
    return out.reshape(own_rows, length, channels)


def normalize(values, axis):
    widened = values.astype(jnp.float32)
    center = widened - jnp.mean(widened, axis=axis, keepdims=True)
    spread = jnp.mean(center * center, axis=axis, keepdims=True)
    return center * lax.rsqrt(spread + epsilon)


def project(normed, weight):
    return jnp.einsum("rkc,cd->rkd", normed, weight, preferred_element_type=jnp.float32)


def split_crop(
    pair_track,
    pair_mask,
    token_mask,
    mult_gate,
    mult_value,
    mult_outgate,
    mult_outproj,
    attn_proj,
    attn_bias,
    attn_outproj,
    trans_gate,
    trans_value,
    trans_outproj,
):
    col_count = lax.axis_size("col")
    rows_here = pair_track.shape[0] // col_count
    full_rows, full_mask = (
        lax.all_to_all(pair_track, "col", split_axis=0, concat_axis=1, tiled=True),
        lax.all_to_all(
            pair_mask.astype(jnp.bfloat16), "col", split_axis=0, concat_axis=1, tiled=True
        ),
    )
    length = full_rows.shape[1]
    row_start = (lax.axis_index("row") * col_count + lax.axis_index("col")) * rows_here
    token_rows = token_mask.astype(jnp.float32)
    own_tokens = lax.dynamic_slice_in_dim(token_rows, row_start, rows_here, 0)
    key_mask = full_mask.astype(jnp.float32) * token_rows[None, :]
    mult_mask = key_mask * own_tokens[:, None]
    residual = full_rows.astype(jnp.float32)
    normed = normalize(full_rows, 2).astype(jnp.bfloat16)
    gate_logit = jnp.einsum("rkc,cd->drk", normed, mult_gate, preferred_element_type=jnp.float32)
    value_part = jnp.einsum("rkc,cd->drk", normed, mult_value, preferred_element_type=jnp.float32)
    hidden = mult_gate.shape[1] // 2
    paired = (jax.nn.sigmoid(gate_logit) * value_part * mult_mask[None]).astype(jnp.bfloat16)
    paired = paired.reshape(2, hidden, rows_here, length)
    spread_pair = lax.all_to_all(paired, "col", split_axis=1, concat_axis=2, tiled=True)
    left_side = spread_pair[0]
    crossed = jnp.einsum(
        "cik,cjk->cij",
        left_side,
        lax.all_gather(spread_pair[1], "row", axis=1, tiled=True),
        preferred_element_type=jnp.float32,
    )
    crossed = crossed.astype(jnp.bfloat16)
    merged = lax.all_to_all(crossed, "col", split_axis=1, concat_axis=0, tiled=True)
    mixed_norm = normalize(merged, 0).astype(jnp.bfloat16)
    update = jnp.einsum("crk,cd->rkd", mixed_norm, mult_outproj, preferred_element_type=jnp.float32)
    outgate = jax.nn.sigmoid(project(normed, mult_outgate))
    residual = residual + outgate * update
    normed = normalize(residual, 2).astype(jnp.bfloat16)
    head_count = attn_bias.shape[1]
    inner_width = attn_outproj.shape[0]
    head_width = inner_width // head_count
    projected = project(normed, attn_proj)
    queries = (projected[:, :, :inner_width] * head_width ** (-0.5)).astype(jnp.bfloat16)
    queries = queries.reshape(rows_here, length, head_count, head_width)
    key_rows = (
        projected[:, :, inner_width : 2 * inner_width]
        .astype(jnp.bfloat16)
        .reshape(rows_here, length, head_count, head_width)
    )
    value_rows = (
        projected[:, :, 2 * inner_width : 3 * inner_width]
        .astype(jnp.bfloat16)
        .reshape(rows_here, length, head_count, head_width)
    )
    gating = jax.nn.sigmoid(projected[:, :, 3 * inner_width :])
    bias_local = jnp.einsum(
        "rkc,ch->hrk", normed, attn_bias, preferred_element_type=jnp.float32
    ).astype(jnp.bfloat16)
    allowed = key_mask > 0.5
    segment = lax.all_gather(bias_local, ("row", "col"), axis=1, tiled=True)
    amount = segment.shape[1]
    scores = jnp.einsum("rjhd,rkhd->hrjk", queries, key_rows, preferred_element_type=jnp.float32)
    scores = scores + segment.astype(jnp.float32)[:, None]
    scores = jnp.where(allowed[None, :, None, :], scores, masked_score)
    row_max = jnp.max(scores, axis=3, keepdims=True)
    expo = jnp.exp(scores - row_max)
    attn_weights = (expo / jnp.sum(expo, axis=3, keepdims=True)).astype(jnp.bfloat16)
    mixed_heads = jnp.einsum(
        "hrjk,rkhd->rjhd", attn_weights, value_rows, preferred_element_type=jnp.float32
    )
    gated_out = (gating * mixed_heads.reshape(rows_here, amount, inner_width)).astype(jnp.bfloat16)
    attended = jnp.einsum(
        "rjd,dc->rjc", gated_out, attn_outproj, preferred_element_type=jnp.float32
    )
    residual = residual + attended
    normed = normalize(residual, 2).astype(jnp.bfloat16)
    transit = (jax.nn.silu(project(normed, trans_gate)) * project(normed, trans_value)).astype(
        jnp.bfloat16
    )
    residual = residual + project(transit, trans_outproj)
    return residual.astype(jnp.bfloat16)


def on_device(pair_track, *others):
    devices = lax.axis_size("row") * lax.axis_size("col")
    pairs = pair_track.shape[0] * pair_track.shape[1] * devices
    heads = others[7].shape[1]
    length = pair_track.shape[1] * lax.axis_size("col")
    fits = pairs * pair_track.shape[2] * 4 <= crop_bytes_max
    tiled = length // devices * pair_track.shape[1] % 16 == 0
    if fits and tiled and heads * length == lanes and pair_track.shape[2] == lanes and devices & (devices - 1) == 0:
        return gathered_crop(pair_track, *others)
    return split_crop(pair_track, *others)


def solution(mesh):
    return jax.shard_map(
        on_device,
        mesh=mesh,
        in_specs=(
            P(("grp", "row"), "col", None),
            P(("grp", "row"), "col"),
            P("grp"),
            P(),
            P(),
            P(),
            P(),
            P(),
            P(),
            P(),
            P(),
            P(),
            P(),
        ),
        out_specs=P(("grp", "row", "col"), None, None),
        check_vma=False,
    )
```

```python
import functools

import jax
import jax.numpy as jnp
from jax import lax
from jax.experimental import pallas as pl
from jax.experimental.pallas import tpu as pltpu
from jax.sharding import PartitionSpec as P

epsilon = 1e-05
masked_score = -1000000000.0
crop_axes = ("row", "col")
lanes = 128
crop_bytes_max = 1 << 20


def dot(left, right):
    return jnp.dot(left, right, preferred_element_type=jnp.float32)


def sigmoid(values):
    return 0.5 * jnp.tanh(0.5 * values) + 0.5


def layer_norm(values):
    center = values - jnp.mean(values, axis=-1, keepdims=True)
    spread = jnp.mean(center * center, axis=-1, keepdims=True)
    return center * lax.rsqrt(spread + epsilon)


def slot_index(offset, devices):
    top = devices.bit_length() - 2
    slot = offset & 1
    for bit in range(1, top + 1):
        slot = slot ^ ((offset >> bit) & 1)
    slot = slot << top
    for bit in range(1, top + 1):
        slot = slot | (((offset >> bit) & 1) << (top - bit))
    return slot


def crop_kernel(
    slots,
    col_count,
    here_ref,
    there_ref,
    token_pair_ref,
    key_place_ref,
    mult_gate_ref,
    mult_value_ref,
    mult_outgate_ref,
    mult_outproj_ref,
    attn_proj_ref,
    attn_bias_ref,
    attn_outproj_ref,
    trans_gate_ref,
    trans_value_ref,
    trans_outproj_ref,
    out_ref,
    crop_ref,
    left,
    right,
    outgate,
    product,
    bias,
    key_lane,
    bias_wide_ref,
):
    channels = outgate.shape[1]
    hidden = mult_outproj_ref.shape[0]
    inner = attn_outproj_ref.shape[0]
    length, spans = bias.shape
    heads = attn_bias_ref.shape[0]
    head_width = inner // heads
    own_rows = out_ref.shape[0] // length
    devices = len(slots)
    row_count = devices // col_count
    block_rows, block_cols = length // row_count, length // col_count
    pairs = block_rows * block_cols
    whole = length * length
    me = lax.axis_index(crop_axes)

    def slot_at(row, col):
        return slot_index((row * col_count + col) ^ me, devices)

    crop_ref[: devices // 2] = here_ref[...]
    crop_ref[devices // 2 :] = there_ref[...]
    packed = jnp.concatenate([here_ref[:, :pairs, :], there_ref[:, :pairs, :]], axis=0).reshape(whole, channels)
    source = layer_norm(packed.astype(jnp.float32)).astype(jnp.bfloat16)
    diagonal = (
        lax.broadcasted_iota(jnp.int32, (block_cols, lanes), 0)
        == lax.broadcasted_iota(jnp.int32, (block_cols, lanes), 1)
    ).astype(jnp.float32)
    masks = []
    for slot, offset in enumerate(slots):
        half_ref = (here_ref, there_ref)[slot // (devices // 2)]
        mask = half_ref[slot % (devices // 2), pairs:, :].astype(jnp.float32)[:block_rows] * token_pair_ref[me ^ offset]
        masks.append((mask[:, None, :] * diagonal[None]).reshape(pairs, lanes))
    mask = dot(jnp.concatenate(masks, axis=0).astype(jnp.bfloat16), jnp.ones((lanes, channels), jnp.bfloat16))
    outgate[...] = sigmoid(dot(source, mult_outgate_ref[...]))
    paired = sigmoid(dot(source, mult_gate_ref[...])) * dot(source, mult_value_ref[...])
    left[...] = (paired[:, :hidden] * mask).astype(jnp.bfloat16).astype(jnp.float32)
    turned = (paired[:, hidden:] * mask).astype(jnp.bfloat16).astype(jnp.float32)
    for slot in range(devices):
        for row in range(block_rows):
            start = slot * pairs + row * block_cols
            right[pl.ds(slot * pairs + row, block_cols, stride=block_rows), :] = turned[start : start + block_cols]

    first_row = me * own_rows
    part = first_row // block_rows
    first_own = first_row - part * block_rows
    own_pairs = own_rows * block_cols
    inside = pl.ds(pl.multiple_of(first_own * block_cols, own_pairs), own_pairs)
    own_slots = [slot_at(part, col) for col in range(col_count)]
    key_mask = jnp.zeros(key_lane.shape, jnp.float32)
    for col in range(col_count):
        mask = crop_ref[own_slots[col], pairs:, :]
        key_mask = key_mask + dot(mask, key_place_ref[col])
    key_lane[...] = key_mask
    head_lanes = (
        lax.broadcasted_iota(jnp.int32, (heads, spans), 0)
        == lax.broadcasted_iota(jnp.int32, (heads, spans), 1) // length
    ).astype(jnp.float32)
    bias_wide_ref[...] = lax.dot_general(
        attn_bias_ref[...].astype(jnp.float32),
        head_lanes,
        (((0,), (0,)), ((), ())),
        preferred_element_type=jnp.float32,
    ).astype(jnp.bfloat16)
    starts = [[slot_at(row, col) * pairs for col in range(col_count)] for row in range(row_count)]

    for part in range(row_count):
        total = [jnp.zeros((length, hidden), jnp.float32) for _ in range(block_rows)]
        for col in range(col_count):
            start = starts[part][col]
            for k in range(block_cols):
                column = jnp.concatenate(
                    [
                        right[pl.ds(pl.multiple_of(starts[row][col] + k * block_rows, block_rows), block_rows), :]
                        for row in range(row_count)
                    ],
                    axis=0,
                )
                for row in range(block_rows):
                    total[row] = total[row] + left[pl.ds(start + row * block_cols + k, 1), :] * column
        step = block_rows * length
        product[pl.ds(pl.multiple_of(part * step, step), step), :] = jnp.concatenate(total, axis=0)

    def absolute(load):
        return jnp.concatenate(
            [
                jnp.concatenate(
                    [load(row, col).reshape(block_rows, block_cols, channels) for col in range(col_count)], axis=1
                )
                for row in range(row_count)
            ],
            axis=0,
        ).reshape(whole, channels)

    def grown(rows, track, gate):
        mixed = layer_norm(rows.astype(jnp.bfloat16).astype(jnp.float32)).astype(jnp.bfloat16)
        rows = track + gate * dot(mixed, mult_outproj_ref[...])
        return rows, layer_norm(rows).astype(jnp.bfloat16)

    def own_block(values):
        values = [value.reshape(own_rows, block_cols, channels) for value in values]
        return jnp.concatenate(values, axis=1).reshape(own_rows * length, channels)

    residual, source = grown(
        product[pl.ds(pl.multiple_of(me * own_rows * length, own_rows * length), own_rows * length), :],
        own_block([crop_ref[slot, inside, :].astype(jnp.float32) for slot in own_slots]),
        own_block(
            [
                outgate[pl.ds(pl.multiple_of(slot * pairs + first_own * block_cols, own_pairs), own_pairs), :]
                for slot in own_slots
            ]
        ),
    )
    projected = dot(source, attn_proj_ref[...])
    queries = (projected[:, :inner] * head_width ** (-0.5)).astype(jnp.bfloat16)
    keys = projected[:, inner : 2 * inner]
    values = projected[:, 2 * inner : 3 * inner]
    gating = sigmoid(projected[:, 3 * inner :])
    head_of_lane = lax.broadcasted_iota(jnp.int32, (1, spans), 1) // length
    head_of_row = lax.broadcasted_iota(jnp.int32, (spans, inner), 0) // length
    head_of_channel = lax.broadcasted_iota(jnp.int32, (spans, inner), 1) // head_width
    same_head = (head_of_row == head_of_channel).astype(jnp.float32)
    _, again = grown(
        product[...],
        absolute(lambda row, col: crop_ref[slot_at(row, col), :pairs, :].astype(jnp.float32)),
        absolute(lambda row, col: outgate[pl.ds(pl.multiple_of(starts[row][col], pairs), pairs), :]),
    )
    key_of_lane = lax.broadcasted_iota(jnp.int32, (length, spans), 1) % length
    on_key = (lax.broadcasted_iota(jnp.int32, (length, spans), 0) == key_of_lane).astype(jnp.float32)
    wide = dot(again, bias_wide_ref[...]).astype(jnp.bfloat16).astype(jnp.float32)
    bias[...] = jnp.sum(wide.reshape(length, length, spans) * on_key[None], axis=1)

    gathered = []
    for row in range(own_rows):
        here = slice(row * length, (row + 1) * length)
        tall_keys = (jnp.concatenate([keys[here]] * heads, axis=0) * same_head).astype(jnp.bfloat16)
        tall_values = (jnp.concatenate([values[here]] * heads, axis=0) * same_head).astype(jnp.bfloat16)
        scores = lax.dot_general(
            queries[here], tall_keys, (((1,), (1,)), ((), ())), preferred_element_type=jnp.float32
        )
        allowed = key_lane[pl.ds(first_own + row, 1), :] > 0.5
        scores = jnp.where(allowed, scores + bias[...], masked_score)
        top = jnp.zeros_like(scores)
        for head in range(heads):
            here_lanes = head_of_lane == head
            most = jnp.max(jnp.where(here_lanes, scores, -jnp.inf), axis=1, keepdims=True)
            top = jnp.where(here_lanes, most, top)
        expo = jnp.exp(scores - top)
        whole = jnp.zeros_like(scores)
        for head in range(heads):
            here_lanes = head_of_lane == head
            amount = jnp.sum(jnp.where(here_lanes, expo, 0.0), axis=1, keepdims=True)
            whole = jnp.where(here_lanes, amount, whole)
        gathered.append(dot((expo / whole).astype(jnp.bfloat16), tall_values))
    gated = (gating * jnp.concatenate(gathered, axis=0)).astype(jnp.bfloat16)
    residual = residual + dot(gated, attn_outproj_ref[...])
    source = layer_norm(residual).astype(jnp.bfloat16)
    gate = dot(source, trans_gate_ref[...])
    transit = (gate * sigmoid(gate) * dot(source, trans_value_ref[...])).astype(jnp.bfloat16)
    out_ref[...] = (residual + dot(transit, trans_outproj_ref[...])).astype(out_ref.dtype)


def gathered_crop(
    pair_track,
    pair_mask,
    token_mask,
    mult_gate,
    mult_value,
    mult_outgate,
    mult_outproj,
    attn_proj,
    attn_bias,
    attn_outproj,
    trans_gate,
    trans_value,
    trans_outproj,
):
    row_count, col_count = lax.axis_size("row"), lax.axis_size("col")
    devices = row_count * col_count
    block_rows, block_cols, channels = pair_track.shape
    length = block_cols * col_count
    pairs = block_rows * block_cols
    below = -(-block_rows // 16) * 16
    own_rows = length // devices
    heads = attn_bias.shape[1]
    spans = heads * length
    padded_mask = jnp.pad(pair_mask, ((pairs, below - block_rows), (0, channels - block_cols)))
    block = jnp.where(
        lax.broadcasted_iota(jnp.int32, (pairs + below, channels), 0) < pairs,
        jnp.pad(pair_track.reshape(pairs, channels), ((0, below), (0, 0))),
        jnp.where(padded_mask > 0, 1, 0).astype(pair_track.dtype),
    )
    crop = block[None]
    slots = [0]
    mask = devices // 2
    while mask:
        turn = mask | 1
        pairing = [(i, i ^ turn) for i in range(devices)]
        parts = 2 if mask > 1 and crop.shape[0] > 2 else 1
        arrived = [lax.ppermute(part, crop_axes, pairing) for part in jnp.split(crop, parts)]
        halves = crop, arrived[0]
        crop = jnp.concatenate([crop] + arrived)
        slots = slots + [slot ^ turn for slot in slots]
        mask //= 2
    tokens = token_mask.astype(jnp.float32)
    token_pair = (
        tokens.reshape(row_count, 1, block_rows, 1) * tokens.reshape(1, col_count, 1, block_cols)
    ).reshape(devices, block_rows, block_cols)
    token_pair = jnp.pad(token_pair, ((0, 0), (0, 0), (0, lanes - block_cols)))
    key_place = (jnp.arange(lanes)[:, None] == jnp.arange(spans)[None, :] % block_cols)[None] & (
        jnp.arange(col_count)[:, None, None] == (jnp.arange(spans) % length // block_cols)[None, None, :]
    )
    key_place = key_place.astype(jnp.bfloat16) * jnp.tile(token_mask, heads).astype(jnp.bfloat16)
    flat = pltpu.VMEM((length * length, channels), jnp.float32)
    tall = pltpu.VMEM((length * length + pairs, channels), jnp.float32)
    out = pl.pallas_call(
        functools.partial(crop_kernel, tuple(slots), col_count),
        out_shape=jax.ShapeDtypeStruct((own_rows * length, channels), jnp.bfloat16),
        in_specs=[pl.BlockSpec(memory_space=pltpu.VMEM)] * 14,
        out_specs=pl.BlockSpec(memory_space=pltpu.VMEM),
        scratch_shapes=[pltpu.VMEM((devices,) + halves[0].shape[1:], halves[0].dtype)]
        + [flat, tall, flat, flat]
        + [pltpu.VMEM((length, spans), jnp.float32), pltpu.VMEM((below, spans), jnp.float32)]
        + [pltpu.VMEM((channels, spans), jnp.bfloat16)],
        compiler_params=pltpu.CompilerParams(vmem_limit_bytes=48 << 20),
        name="crop",
    )(
        *halves,
        token_pair,
        key_place,
        mult_gate,
        mult_value,
        mult_outgate,
        mult_outproj,
        attn_proj,
        attn_bias.T,
        attn_outproj,
        trans_gate,
        trans_value,
        trans_outproj,
    )
    return out.reshape(own_rows, length, channels)


def normalize(values, axis):
    widened = values.astype(jnp.float32)
    center = widened - jnp.mean(widened, axis=axis, keepdims=True)
    spread = jnp.mean(center * center, axis=axis, keepdims=True)
    return center * lax.rsqrt(spread + epsilon)


def project(normed, weight):
    return jnp.einsum("rkc,cd->rkd", normed, weight, preferred_element_type=jnp.float32)


def split_crop(
    pair_track,
    pair_mask,
    token_mask,
    mult_gate,
    mult_value,
    mult_outgate,
    mult_outproj,
    attn_proj,
    attn_bias,
    attn_outproj,
    trans_gate,
    trans_value,
    trans_outproj,
):
    col_count = lax.axis_size("col")
    rows_here = pair_track.shape[0] // col_count
    full_rows, full_mask = (
        lax.all_to_all(pair_track, "col", split_axis=0, concat_axis=1, tiled=True),
        lax.all_to_all(
            pair_mask.astype(jnp.bfloat16), "col", split_axis=0, concat_axis=1, tiled=True
        ),
    )
    length = full_rows.shape[1]
    row_start = (lax.axis_index("row") * col_count + lax.axis_index("col")) * rows_here
    token_rows = token_mask.astype(jnp.float32)
    own_tokens = lax.dynamic_slice_in_dim(token_rows, row_start, rows_here, 0)
    key_mask = full_mask.astype(jnp.float32) * token_rows[None, :]
    mult_mask = key_mask * own_tokens[:, None]
    residual = full_rows.astype(jnp.float32)
    normed = normalize(full_rows, 2).astype(jnp.bfloat16)
    gate_logit = jnp.einsum("rkc,cd->drk", normed, mult_gate, preferred_element_type=jnp.float32)
    value_part = jnp.einsum("rkc,cd->drk", normed, mult_value, preferred_element_type=jnp.float32)
    hidden = mult_gate.shape[1] // 2
    paired = (jax.nn.sigmoid(gate_logit) * value_part * mult_mask[None]).astype(jnp.bfloat16)
    paired = paired.reshape(2, hidden, rows_here, length)
    spread_pair = lax.all_to_all(paired, "col", split_axis=1, concat_axis=2, tiled=True)
    left_side = spread_pair[0]
    crossed = jnp.einsum(
        "cik,cjk->cij",
        left_side,
        lax.all_gather(spread_pair[1], "row", axis=1, tiled=True),
        preferred_element_type=jnp.float32,
    )
    crossed = crossed.astype(jnp.bfloat16)
    merged = lax.all_to_all(crossed, "col", split_axis=1, concat_axis=0, tiled=True)
    mixed_norm = normalize(merged, 0).astype(jnp.bfloat16)
    update = jnp.einsum("crk,cd->rkd", mixed_norm, mult_outproj, preferred_element_type=jnp.float32)
    outgate = jax.nn.sigmoid(project(normed, mult_outgate))
    residual = residual + outgate * update
    normed = normalize(residual, 2).astype(jnp.bfloat16)
    head_count = attn_bias.shape[1]
    inner_width = attn_outproj.shape[0]
    head_width = inner_width // head_count
    projected = project(normed, attn_proj)
    queries = (projected[:, :, :inner_width] * head_width ** (-0.5)).astype(jnp.bfloat16)
    queries = queries.reshape(rows_here, length, head_count, head_width)
    key_rows = (
        projected[:, :, inner_width : 2 * inner_width]
        .astype(jnp.bfloat16)
        .reshape(rows_here, length, head_count, head_width)
    )
    value_rows = (
        projected[:, :, 2 * inner_width : 3 * inner_width]
        .astype(jnp.bfloat16)
        .reshape(rows_here, length, head_count, head_width)
    )
    gating = jax.nn.sigmoid(projected[:, :, 3 * inner_width :])
    bias_local = jnp.einsum(
        "rkc,ch->hrk", normed, attn_bias, preferred_element_type=jnp.float32
    ).astype(jnp.bfloat16)
    allowed = key_mask > 0.5
    segment = lax.all_gather(bias_local, ("row", "col"), axis=1, tiled=True)
    amount = segment.shape[1]
    scores = jnp.einsum("rjhd,rkhd->hrjk", queries, key_rows, preferred_element_type=jnp.float32)
    scores = scores + segment.astype(jnp.float32)[:, None]
    scores = jnp.where(allowed[None, :, None, :], scores, masked_score)
    row_max = jnp.max(scores, axis=3, keepdims=True)
    expo = jnp.exp(scores - row_max)
    attn_weights = (expo / jnp.sum(expo, axis=3, keepdims=True)).astype(jnp.bfloat16)
    mixed_heads = jnp.einsum(
        "hrjk,rkhd->rjhd", attn_weights, value_rows, preferred_element_type=jnp.float32
    )
    gated_out = (gating * mixed_heads.reshape(rows_here, amount, inner_width)).astype(jnp.bfloat16)
    attended = jnp.einsum(
        "rjd,dc->rjc", gated_out, attn_outproj, preferred_element_type=jnp.float32
    )
    residual = residual + attended
    normed = normalize(residual, 2).astype(jnp.bfloat16)
    transit = (jax.nn.silu(project(normed, trans_gate)) * project(normed, trans_value)).astype(
        jnp.bfloat16
    )
    residual = residual + project(transit, trans_outproj)
    return residual.astype(jnp.bfloat16)


def on_device(pair_track, *others):
    devices = lax.axis_size("row") * lax.axis_size("col")
    pairs = pair_track.shape[0] * pair_track.shape[1] * devices
    heads = others[7].shape[1]
    length = pair_track.shape[1] * lax.axis_size("col")
    fits = pairs * pair_track.shape[2] * 4 <= crop_bytes_max
    tiled = length // devices * pair_track.shape[1] % 16 == 0
    if fits and tiled and heads * length == lanes and pair_track.shape[2] == lanes and devices & (devices - 1) == 0:
        return gathered_crop(pair_track, *others)
    return split_crop(pair_track, *others)


def solution(mesh):
    return jax.shard_map(
        on_device,
        mesh=mesh,
        in_specs=(
            P(("grp", "row"), "col", None),
            P(("grp", "row"), "col"),
            P("grp"),
            P(),
            P(),
            P(),
            P(),
            P(),
            P(),
            P(),
            P(),
            P(),
            P(),
        ),
        out_specs=P(("grp", "row", "col"), None, None),
        check_vma=False,
    )
```
